128 devices in a mesh: row: 8 (over y_lo, z), stop: 16 (over y_hi, x, core).
Axes of the slice: x: 4, y: 4 (y_hi: 2, y_lo: 2; y = y_hi * 2 + y_lo), z: 4, core: 2. Of those that a mesh axis runs over, the one named last changes fastest.
Arguments:
- radiosity: bfloat16 [32, 1024, 256], P('row', 'stop'), may hold values from -6 to 6
- emission: bfloat16 [32, 1024, 256], P('row', 'stop'), may hold values from -6 to 6
- areas: float32 [32, 1024], P('row', 'stop'), may hold values from 0.25 to 4
- patch_material: int32 [32, 1024], P('row', 'stop'), may hold values from 0 to 15
- reflect_table: float32 [16, 32], replicated, may hold values from 0.2 to 0.95
- pair_blocks: bfloat16 [32, 16, 1024, 1024], P('row', 'stop'), may hold values from 0.0005493164 to 0.016479492
- far_blocks: bfloat16 [32, 1024, 1024], P('row', 'stop'), may hold values from 0.0005493164 to 0.016479492
Outputs:
- updated: float32 [32, 1024, 256], P('row', 'stop')
The draws below stay inside these ranges and needn't reach their ends.
All inputs are finite; a program needn't handle non-finite values.
Results may differ from the reference program's by a relative error of at most 0.0003.
Values may be sent and summed in bfloat16 or wider, within the bound.
A program may use at most 192 MiB of HBM per device.

```python
import math
import jax
import jax.numpy as jnp
from jax import lax

BANDS = 32
CASES = 8
PB = 1024
MATERIALS = 16
K = 32
OFFSETS = 16


def set_ends(array, stream_key, least, largest):
    index_at = [jax.random.randint(jax.random.fold_in(stream_key, axis), (), 0, length) for axis, length in enumerate(array.shape)]
    main_axis = array.shape.index(max(array.shape))
    neighbour = index_at[:main_axis] + [(index_at[main_axis] + 1) % array.shape[main_axis]] + index_at[main_axis + 1:]
    return array.at[tuple(index_at)].set(least).at[tuple(neighbour)].set(largest)


def block_levels(own_key, shape, split, low, top_value):
    def one(position, blocks):
        heights = jax.random.uniform(jax.random.fold_in(jax.random.fold_in(own_key, 6), position), (blocks,), jnp.float32, low / len(split), top_value / len(split))
        return jnp.repeat(jnp.exp(heights), shape[position] // blocks).reshape((-1,) + (1,) * (len(shape) - position - 1))

    gain = one(*split[0])
    for cut in split[1:]:
        gain = gain * one(*cut)
    return gain


def scatter_about(own_key, dims, deviation, most, split=(), kind=jnp.bfloat16):
    drawn = deviation * jax.random.normal(own_key, dims, jnp.float32)
    if split:
        drawn = drawn * block_levels(own_key, dims, split, -0.22, 0.18)
    return jnp.clip(drawn, -most, most).astype(kind)


def setup_inputs(seed: int = 0) -> dict:
    keys = jax.random.split(jax.random.key(seed), 8)
    return {
        "radiosity": scatter_about(keys[0], (K, PB, BANDS * CASES), 1.0, 6.0, ((0, 8), (1, 16))),
        "emission": scatter_about(keys[1], (K, PB, BANDS * CASES), 1.0, 6.0, ((0, 8), (1, 16))),
        "areas": jnp.clip(jnp.exp(math.log(4.0) - 2.7725887 * jax.random.uniform(keys[2], (K, PB), jnp.float32) ** block_levels(keys[2], (K, PB), ((0, 8), (1, 16)), -0.2, 0.2)), 0.25, 4.0),
        "patch_material": set_ends(jax.random.randint(keys[3], (K, PB), 0, MATERIALS), jax.random.fold_in(keys[3], 1), 0, MATERIALS - 1).astype(jnp.int32),
        "reflect_table": jnp.clip(jnp.exp(jax.random.uniform(keys[4], (MATERIALS, BANDS), jnp.float32, math.log(0.2), math.log(0.95))), 0.2, 0.95),
        "pair_blocks": jnp.clip(jnp.exp(math.log(0.016479492) - 3.4011974 * jax.random.uniform(keys[5], (K, OFFSETS, PB, PB), jnp.float32) ** block_levels(keys[5], (K, OFFSETS, PB, PB), ((0, 8), (1, 16)), -0.2, 0.2)), 0.0005493164, 0.016479492).astype(jnp.bfloat16),
        "far_blocks": jnp.clip(jnp.exp(math.log(0.016479492) - 3.4011974 * jax.random.uniform(keys[6], (K, PB, PB), jnp.float32) ** block_levels(keys[6], (K, PB, PB), ((0, 8), (1, 16)), -0.2, 0.2)), 0.0005493164, 0.016479492).astype(jnp.bfloat16),
    }


def reference(radiosity, emission, areas, patch_material, reflect_table, pair_blocks, far_blocks):
    source = radiosity.astype(jnp.float32)

    def offset_step(total, offset):
        blocks = lax.dynamic_index_in_dim(pair_blocks, offset, 1, keepdims=False).astype(jnp.float32)
        ahead = jnp.roll(source, -offset, axis=0)
        forward = jnp.einsum("bij,bjc->bic", blocks, ahead)
        mirrored = jnp.einsum("bji,bjc->bic", blocks, source)
        return total + forward + jnp.roll(mirrored, offset, axis=0), None

    start = jnp.zeros(source.shape, jnp.float32)
    total, _ = lax.scan(offset_step, start, jnp.arange(OFFSETS, dtype=jnp.int32))
    opposite = jnp.roll(source, -(K // 2), axis=0)
    total = total + jnp.einsum("bij,bjc->bic", far_blocks.astype(jnp.float32), opposite)
    irradiation = total / areas[..., None]
    onehot = (patch_material[..., None] == jnp.arange(MATERIALS, dtype=jnp.int32)).astype(jnp.float32)
    reflect = jnp.einsum("bim,mn->bin", onehot, reflect_table, precision=lax.Precision.HIGHEST)
    reflect = jnp.tile(reflect, (1, 1, CASES))
    return emission.astype(jnp.float32) + reflect * irradiation
```

```python
import functools

import jax
import jax.numpy as jnp
from jax import lax
from jax.experimental import pallas as pl
from jax.experimental.pallas import tpu as pltpu
from jax.sharding import PartitionSpec as P

MESH = pl.DeviceIdType.MESH
F32 = jnp.float32


class Links:
    def __init__(self, send_sem, recv_sem):
        self.send_sem, self.recv_sem = send_sem, recv_sem
        self.names, self.recv_count, self.sent = {}, 0, []

    def name(self, key, count=1):
        self.names[key] = self.recv_count
        self.recv_count += count

    def copy(self, key, src, dst, target, extra=0):
        made = pltpu.make_async_remote_copy(
            src_ref=src,
            dst_ref=dst,
            send_sem=self.send_sem.at[len(self.sent)],
            recv_sem=self.recv_sem.at[self.names[key] + extra],
            device_id=target,
            device_id_type=MESH,
        )
        self.sent.append(made)
        return made

    def send(self, key, src, dst, target, extra=0):
        self.copy(key, src, dst, target, extra).start()

    def arrived(self, key, dst, target, extra=0):
        pltpu.make_async_remote_copy(
            src_ref=dst,
            dst_ref=dst,
            send_sem=self.send_sem.at[0],
            recv_sem=self.recv_sem.at[self.names[key] + extra],
            device_id=target,
            device_id_type=MESH,
        ).wait_recv()


def kernel(
    rows, columns,
    rad, emi, area, mat, tab, pair, far, out,
    blocks, own, win, grp, fbuf, rf, fw, fs, fy, fx, mr, ms, un, mx, hz_own, hz, emi_v,
    send_sem, recv_sem, local_sem,
):
    nq, slice_rows, width = rad.shape
    patches = pair.shape[2]
    half_patches = patches // 2
    slots = nq + 1
    groups = 2 * columns + nq - 1
    parts = [(g * nq, min(nq, groups - g * nq)) for g in range(-(-groups // nq))]
    row, stop = lax.axis_index("row"), lax.axis_index("stop")
    half, col, core = stop // (2 * columns), (stop // 2) % columns, stop % 2
    others = range(1, columns)

    def at(row_by, half_to, col_to, core_to):
        return (row_by, half_to * (2 * columns) + col_to * 2 + core_to)

    def row_up(by):
        return lax.rem(row + by, rows)

    def row_down(by):
        return lax.rem(row + rows - by, rows)

    def col_up(by):
        return lax.rem(col + by, columns)

    def col_down(by):
        return lax.rem(col + columns - by, columns)

    sibling = at(row, half, col, 1 - core)
    partner = at(row, 1 - half, col, core)
    me_col = {by: at(row, half, col_up(by), core) for by in others}

    links = Links(send_sem, recv_sem)
    for by in others:
        for key in ("own_x", "rf_x", "win_x"):
            links.name((key, by))
        for i in range(slots):
            links.name(("mx", by, i))
        for q in range(nq):
            links.name(("fx", by, q))
    for by in range(columns):
        for key in ("own_y", "own_sx", "own_sy", "rf_s", "win_s"):
            links.name((key, by))
    links.name("rf")
    links.name("far_y")
    for g in range(len(parts)):
        links.name(("grp", g), 2)
        links.name(("hz", g), 2)
    for q in range(nq):
        for key in ("ms", "fs", "fy"):
            links.name((key, q))

    local_count = [0]

    def local(src, dst):
        made = pltpu.make_async_copy(src, dst, local_sem.at[local_count[0]])
        local_count[0] += 1
        return made

    own_copy = local(rad, own.at[:, half, col, core])
    own_copy.start()
    rows_of_far = pl.ds(pl.multiple_of(half * half_patches, half_patches), half_patches)
    rows_of_other = pl.ds(pl.multiple_of((1 - half) * half_patches, half_patches), half_patches)
    block_copies = []
    for q in range(nq):
        made = local(pair.at[q, 0], blocks.at[q])
        made.start()
        block_copies.append(made)
    far_copy = local(far.at[:, :, rows_of_far], fbuf.at[half])
    far_copy.start()
    emi_copy = local(emi, emi_v)
    emi_copy.start()

    barrier = pltpu.get_barrier_semaphore()
    peers = [sibling] + [me_col[by] for by in others]
    for by in range(rows):
        for flip in range(2):
            if by or flip:
                peers.append(at(row_up(by), half if flip == 0 else 1 - half, col, core))
    for peer in peers:
        pl.semaphore_signal(barrier, inc=1, device_id=peer, device_id_type=MESH)
    pl.semaphore_wait(barrier, len(peers))

    for by in others:
        links.send(("own_x", by), rad, own.at[:, half, col, core], me_col[by])
    links.send(("own_y", 0), rad, own.at[:, half, col, core], partner)
    links.send("rf", rad, rf.at[:, col, core], at(row_down(rows // 2), half, col, core))
    self_grp = None
    for half_to in range(2):
        for g, (first, count) in enumerate(parts):
            by = half_to * (2 * columns) // nq + g
            src = rad.at[pl.ds(0, count)]
            dst = grp.at[pl.ds(first, count), half]
            remote = links.copy(("grp", g), src, dst, at(row_down(by), half_to, col, core), half)
            if by == 0:
                self_grp = (remote, local(src, dst))

                @pl.when(half == 1)
                def _(remote=remote):
                    remote.start()

                @pl.when(half == 0)
                def _(near=self_grp[1]):
                    near.start()
            else:
                remote.start()
    links.send("far_y", far.at[:, :, rows_of_other], fbuf.at[half], partner)
    links.send(("own_sx", 0), rad, own.at[:, half, col, core], sibling)

    for by in others:
        src_col = col_down(by)
        piece = own.at[:, half, src_col, core]
        links.arrived(("own_x", by), piece, me_col[by])
        links.send(("own_y", by), piece, piece, partner)
        links.send(("own_sx", by), piece, piece, sibling)

    piece = rf.at[:, col, core]
    links.arrived("rf", piece, sibling)
    for by in others:
        links.send(("rf_x", by), piece, piece, me_col[by])
    links.send(("rf_s", 0), piece, piece, sibling)

    for half_from in range(2):
        for g, (first, count) in enumerate(parts):
            piece = grp.at[pl.ds(first, count), half_from]
            if g == 0 and half_from == 0:

                @pl.when(half == 1)
                def _(piece=piece):
                    links.arrived(("grp", 0), piece, sibling, 0)

                @pl.when(half == 0)
                def _():
                    self_grp[1].wait()
            else:
                links.arrived(("grp", g), piece, sibling, half_from)
    for by in others:
        links.send(
            ("win_x", by),
            grp.at[pl.ds(2 * col_up(by), slots)],
            win.at[:, :, col, core],
            me_col[by],
        )
    win_copy = local(grp.at[pl.ds(2 * col, slots)], win.at[:, :, col, core])
    win_copy.start()
    links.send(
        ("win_s", 0),
        grp.at[pl.ds(2 * col + 1 - core, nq)],
        win.at[pl.ds(1 - core, nq), :, col, core],
        sibling,
    )

    for by in range(columns):
        src_col = col_down(by)
        piece = own.at[:, 1 - half, src_col, core]
        links.arrived(("own_y", by), piece, partner)
        links.send(("own_sy", by), piece, piece, sibling)

    own_copy.wait()
    for by in range(columns):
        src_col = col_down(by)
        links.arrived(("own_sx", by), own.at[:, half, src_col, 1 - core], sibling)
        links.arrived(("own_sy", by), own.at[:, 1 - half, src_col, 1 - core], sibling)

    per_tile = columns // 2
    tile = per_tile * 2 * slice_rows
    tiles = patches // tile

    def tile_at(n):
        return pl.ds(pl.multiple_of(n * tile, tile), tile)

    for q in range(nq):
        block_copies[q].wait()

        def mirrored(n, carry, q=q):
            product = lax.dot_general(
                blocks[q, :, tile_at(n)],
                own[q].reshape(patches, width),
                (((0,), (0,)), ((), ())),
                preferred_element_type=F32,
            )
            mr[q, n // 2, pl.ds((n % 2) * per_tile, per_tile)] = product.reshape(
                per_tile, 2, slice_rows, width
            )
            return carry

        lax.fori_loop(0, tiles, mirrored, 0)
        links.send(("ms", q), mr.at[q, :, :, 1 - core], ms.at[q], sibling)

    for i in range(slots):
        if i < nq:
            links.arrived(("ms", i), ms.at[i], sibling)
        if i == 0:

            @pl.when(core == 0)
            def _():
                un[0] = mr[0, :, :, 0]

            @pl.when(core == 1)
            def _():
                un[0] = ms[0]
        elif i == nq:

            @pl.when(core == 0)
            def _():
                un[nq] = ms[nq - 1]

            @pl.when(core == 1)
            def _():
                un[nq] = mr[nq - 1, :, :, 1]
        else:
            un[i] = mr[i - core, :, :, core] + ms[i - 1 + core]
        for by in others:
            links.send(
                ("mx", by, i), un.at[i, :, col_up(by)], mx.at[by - 1, i], me_col[by]
            )

    for by in others:
        piece = rf.at[:, col_down(by), core]
        links.arrived(("rf_x", by), piece, sibling)
        links.send(("rf_s", by), piece, piece, sibling)
    for by in others:
        src_col = col_down(by)
        links.arrived(("win_x", by), win.at[:, :, src_col, core], sibling)
        piece = win.at[pl.ds(1 - core, nq), :, src_col, core]
        links.send(("win_s", by), piece, piece, sibling)

    win_copy.wait()
    for by in range(columns):
        src_col = col_down(by)
        links.arrived(
            ("win_s", by), win.at[pl.ds(core, nq), :, src_col, 1 - core], sibling
        )
    for q in range(nq):

        def forward(n, carry, q=q):
            product = jnp.dot(
                blocks[q, tile_at(n), :],
                win[core + q].reshape(patches, width),
                preferred_element_type=F32,
            )
            fw[q, n // 2, pl.ds((n % 2) * per_tile, per_tile)] = product.reshape(
                per_tile, 2, slice_rows, width
            )
            return carry

        lax.fori_loop(0, tiles, forward, 0)
        links.send(("fs", q), fw.at[q, :, :, 1 - core], fs.at[q], sibling)

    for by in range(columns):
        links.arrived(("rf_s", by), rf.at[:, col_down(by), 1 - core], sibling)
    far_copy.wait()
    links.arrived("far_y", fbuf.at[1 - half], partner)
    for q in range(nq):
        links.arrived(("fs", q), fs.at[q], sibling)
        fw[q, :, :, core] = fw[q, :, :, core] + fs[q]
        opposite = jnp.dot(
            fbuf[:, q].reshape(2 * slice_rows, half_patches),
            rf[q].reshape(half_patches, width),
            preferred_element_type=F32,
        )
        fw[q, :, col, core] = fw[q, :, col, core] + opposite.reshape(2, slice_rows, width)
        links.send(("fy", q), fw.at[q, 1 - half, :, core], fy.at[q], partner)

    for q in range(nq):
        links.arrived(("fy", q), fy.at[q], partner)
        fw[q, half, :, core] = fw[q, half, :, core] + fy[q]
        for by in others:
            links.send(
                ("fx", by, q), fw.at[q, half, col_up(by), core], fx.at[by - 1, q], me_col[by]
            )

    hz_own[...] = jnp.zeros_like(hz_own)
    hz_own[pl.ds(2 * col, slots)] = un[:, :, col]
    for by in others:
        src_col = col_down(by)
        for i in range(slots):
            links.arrived(("mx", by, i), mx.at[by - 1, i], sibling)
        reach = pl.ds(2 * src_col, slots)
        hz_own[reach] = hz_own[reach] + mx[by - 1]
    self_hz = None
    first_row = half * (2 * columns) // nq
    for half_to in range(2):
        for g, (first, count) in enumerate(parts):
            src = hz_own.at[pl.ds(first, count), half_to]
            dst = hz.at[half, pl.ds(first, count)]
            target = at(row_up(first_row + g), half_to, col, core)
            remote = links.copy(("hz", g), src, dst, target, half)
            if g == 0 and half_to == 0:
                self_hz = (remote, local(src, dst))

                @pl.when(half == 1)
                def _(remote=remote):
                    remote.start()

                @pl.when(half == 0)
                def _(near=self_hz[1]):
                    near.start()
            else:
                remote.start()

    emi_copy.wait()
    for by in others:
        for q in range(nq):
            links.arrived(("fx", by, q), fx.at[by - 1, q], sibling)
    for half_from in range(2):
        for g, (first, count) in enumerate(parts):
            piece = hz.at[half_from, pl.ds(first, count)]
            if g == 0 and half_from == 0:

                @pl.when(half == 1)
                def _(piece=piece):
                    links.arrived(("hz", 0), piece, sibling, 0)

                @pl.when(half == 0)
                def _():
                    self_hz[1].wait()
            else:
                links.arrived(("hz", g), piece, sibling, half_from)

    kinds, bands = tab.shape
    reflect_of = jnp.concatenate([tab[...]] * (width // bands), axis=1)
    across = lax.broadcasted_iota(jnp.int32, (slice_rows, slice_rows), 1)
    down = lax.broadcasted_iota(jnp.int32, (slice_rows, slice_rows), 0)

    def upright(values):
        spread = jnp.broadcast_to(values, (slice_rows, slice_rows))
        return jnp.sum(jnp.where(across == down, spread, 0), axis=1, keepdims=True)

    for q in range(nq):
        total = fw[q, half, col, core]
        for by in others:
            total = total + fx[by - 1, q]
        for half_from in range(2):
            for u in range(q, groups, nq):
                total = total + hz[half_from, u]
        kind = upright(mat[pl.ds(q, 1), :])
        reflect = jnp.zeros((slice_rows, width), F32)
        for m in range(kinds):
            reflect = jnp.where(kind == m, reflect_of[m : m + 1, :], reflect)
        irradiation = total / upright(area[pl.ds(q, 1), :])
        out[q] = emi_v[q].astype(F32) + reflect * irradiation

    conditional = (self_grp[0], self_hz[0])
    for made in links.sent:
        if made is conditional[0] or made is conditional[1]:

            @pl.when(half == 1)
            def _(made=made):
                made.wait_send()
        else:
            made.wait_send()


def on_device(rows, columns, radiosity, emission, areas, patch_material, reflect_table, pair_blocks, far_blocks):
    nq, slice_rows, width = radiosity.shape
    patches = pair_blocks.shape[2]
    slots = nq + 1
    groups = 2 * columns + nq - 1
    half_patches = patches // 2
    bf16 = jnp.bfloat16
    scratch = [
        pltpu.VMEM((nq, patches, patches), bf16),
        pltpu.VMEM((nq, 2, columns, 2, slice_rows, width), bf16),
        pltpu.VMEM((slots, 2, columns, 2, slice_rows, width), bf16),
        pltpu.VMEM((groups, 2, slice_rows, width), bf16),
        pltpu.VMEM((2, nq, slice_rows, half_patches), bf16),
        pltpu.VMEM((nq, columns, 2, slice_rows, width), bf16),
        pltpu.VMEM((nq, 2, columns, 2, slice_rows, width), F32),
        pltpu.VMEM((nq, 2, columns, slice_rows, width), F32),
        pltpu.VMEM((nq, columns, slice_rows, width), F32),
        pltpu.VMEM((columns - 1, nq, slice_rows, width), F32),
        pltpu.VMEM((nq, 2, columns, 2, slice_rows, width), F32),
        pltpu.VMEM((nq, 2, columns, slice_rows, width), F32),
        pltpu.VMEM((slots, 2, columns, slice_rows, width), F32),
        pltpu.VMEM((columns - 1, slots, 2, slice_rows, width), F32),
        pltpu.VMEM((groups, 2, slice_rows, width), F32),
        pltpu.VMEM((2, groups, slice_rows, width), F32),
        pltpu.VMEM((nq, slice_rows, width), bf16),
        pltpu.SemaphoreType.DMA((160,)),
        pltpu.SemaphoreType.DMA((160,)),
        pltpu.SemaphoreType.DMA((16,)),
    ]
    any_space = pl.BlockSpec(memory_space=pl.ANY)
    vmem = pl.BlockSpec(memory_space=pltpu.VMEM)
    flops = 4 * nq * patches * patches * width
    return pl.pallas_call(
        functools.partial(kernel, rows, columns),
        out_shape=jax.ShapeDtypeStruct((nq, slice_rows, width), F32),
        in_specs=[any_space, any_space, vmem, vmem, vmem, any_space, any_space],
        out_specs=vmem,
        scratch_shapes=scratch,
        compiler_params=pltpu.CompilerParams(
            collective_id=0, has_side_effects=True, vmem_limit_bytes=58 * 2**20
        ),
        cost_estimate=pl.CostEstimate(
            flops=flops, bytes_accessed=2 * nq * patches * patches, transcendentals=0
        ),
    )(radiosity, emission, areas, patch_material, reflect_table, pair_blocks, far_blocks)


def solution(mesh):
    rows, stops = mesh.shape["row"], mesh.shape["stop"]
    return jax.shard_map(
        functools.partial(on_device, rows, stops // 4),
        mesh=mesh,
        in_specs=(
            P("row", "stop", None),
            P("row", "stop", None),
            P("row", "stop"),
            P("row", "stop"),
            P(),
            P("row", "stop", None, None),
            P("row", "stop", None),
        ),
        out_specs=P("row", "stop", None),
        check_vma=False,
    )
```

```python
import functools

import jax
import jax.numpy as jnp
from jax import lax
from jax.experimental import pallas as pl
from jax.experimental.pallas import tpu as pltpu
from jax.sharding import PartitionSpec as P

MESH = pl.DeviceIdType.MESH
F32 = jnp.float32


SPLIT = 0
XFIRST = ()
QORDER = (0, 1, 2, 3)
ORDER = (
    "own_send",
    "reach_send 0",
    "reach_send 1",
    "own_pass_y",
    "own_pass_x",
    "reach_pass 0",
    "own_end",
    "reach_pass 1",
    "opposite_send",
    "mirror",
    "unite",
    "opposite_pass",
    "window_pass",
    "sums_send 0",
    "sums_send 1",
    "far_send",
    "sums_send 2",
    "sums_send 3",
    "forward",
    "forward_unite 0",
    "forward_unite 1",
    "forward_unite 2",
    "forward_unite 3",
    "opposite 0",
    "opposite 1",
    "opposite 2",
    "opposite 3",
    "sums_pass 0",
    "forward_pass 0",
    "sums_pass 1",
    "forward_pass 1",
    "sums_pass 2",
    "forward_pass 2",
    "sums_pass 3",
    "forward_pass 3",
)


class Links:
    def __init__(self, send_sem, recv_sem):
        self.send_sem, self.recv_sem = send_sem, recv_sem
        self.names, self.recv_count, self.sent = {}, 0, []

    def name(self, key, count=1):
        self.names[key] = self.recv_count
        self.recv_count += count

    def copy(self, key, src, dst, target, extra=0):
        made = pltpu.make_async_remote_copy(
            src_ref=src,
            dst_ref=dst,
            send_sem=self.send_sem.at[len(self.sent)],
            recv_sem=self.recv_sem.at[self.names[key] + extra],
            device_id=target,
            device_id_type=MESH,
        )
        self.sent.append(made)
        return made

    def send(self, key, src, dst, target, extra=0):
        self.copy(key, src, dst, target, extra).start()

    def arrived(self, key, dst, target, extra=0):
        pltpu.make_async_remote_copy(
            src_ref=dst,
            dst_ref=dst,
            send_sem=self.send_sem.at[0],
            recv_sem=self.recv_sem.at[self.names[key] + extra],
            device_id=target,
            device_id_type=MESH,
        ).wait_recv()


def kernel(
    rows, columns,
    rad, emi, area, mat, tab, pair, far, out,
    blocks, own, win, grp, fbuf, rf, fw, fs, fy, fx, mr, ms, un, mx, hz_own, hz, emi_v, refl,
    send_sem, recv_sem, local_sem,
):
    nq, slice_rows, width = rad.shape
    patches = pair.shape[2]
    half_patches = patches // 2
    slots = nq + 1
    groups = 2 * columns + nq - 1
    parts = [(g * nq, min(nq, groups - g * nq)) for g in range(-(-groups // nq))]
    row, stop = lax.axis_index("row"), lax.axis_index("stop")
    half, col, core = stop // (2 * columns), (stop // 2) % columns, stop % 2
    others = range(1, columns)

    def at(row_by, half_to, col_to, core_to):
        return (row_by, half_to * (2 * columns) + col_to * 2 + core_to)

    def row_up(by):
        return lax.rem(row + by, rows)

    def row_down(by):
        return lax.rem(row + rows - by, rows)

    def col_up(by):
        return lax.rem(col + by, columns)

    def col_down(by):
        return lax.rem(col + columns - by, columns)

    sibling = at(row, half, col, 1 - core)
    partner = at(row, 1 - half, col, core)
    me_col = {by: at(row, half, col_up(by), core) for by in others}
    starts = (0, 2 * columns // nq)
    halves = (half, 1 - half)

    def start_of(which):
        return jnp.where(which == 0, starts[0], starts[1])

    split = SPLIT
    links = Links(send_sem, recv_sem)
    for by in others:
        for key in ("own_x", "own_sx", "own_ya", "own_xb", "own_sa", "own_sb"):
            links.name((key, by))
        for flip in range(2):
            links.name(("far", by, flip))
            links.name(("win_x", by, flip))
        for part in range(4):
            links.name(("mx", by, part))
        for q in range(nq):
            links.name(("fx", by, q))
    for by in range(columns):
        links.name(("win_s", by))
    for key in ("own_s", "own_y", "own_sy"):
        links.name((key, 0))
    for key in ("rf", "rf_s"):
        links.name((key, 0), 2)
    for g in range(len(parts)):
        for flip in range(2):
            links.name(("grp", g, flip))
        for part in range(4):
            links.name(("hz", g, part))
    for q in range(nq):
        for key in ("ms", "fs", "fy"):
            links.name((key, q))

    local_count = [0]

    def local(src, dst):
        made = pltpu.make_async_copy(src, dst, local_sem.at[local_count[0]])
        local_count[0] += 1
        return made

    def far_columns(side, column):
        first = side * half_patches + column * (2 * slice_rows)
        return pl.ds(pl.multiple_of(first, 2 * slice_rows), 2 * slice_rows)

    def offsets(mine, theirs):
        reach = {starts[mine] + g for g in range(len(parts))}
        back = {-(starts[theirs] + g) for g in range(len(parts))}
        both = {by % rows for by in reach | back | {rows // 2}}
        return sorted(both - {0} if mine == theirs else both)

    barrier = pltpu.get_barrier_semaphore()
    peers = []
    for a, b in zip(offsets(0, 1), offsets(1, 0), strict=True):
        peers.append(at(row_up(jnp.where(half == 0, a, b)), 1 - half, col, core))
    for a, b in zip(offsets(0, 0), offsets(1, 1), strict=True):
        peers.append(at(row_up(jnp.where(half == 0, a, b)), half, col, core))
    peers += [me_col[by] for by in others] + [sibling]
    for peer in peers:
        pl.semaphore_signal(barrier, inc=1, device_id=peer, device_id_type=MESH)

    own_copy = local(rad, own.at[:, half, col, core])
    own_copy.start()
    block_copies = []
    for q in range(nq):
        made = local(pair.at[q, 0], blocks.at[q])
        made.start()
        block_copies.append(made)
    far_copies = []
    for side in range(2):
        made = local(far.at[:, :, far_columns(side, col)], fbuf.at[side, :, col])
        made.start()
        far_copies.append(made)
    emi_copy = local(emi, emi_v)
    emi_copy.start()
    pl.semaphore_wait(barrier, len(peers))

    mine = own.at[:, half, col, core]
    win_copies, conditional = [], []
    a_part, b_part = pl.ds(0, split), pl.ds(split, nq - split)
    per_tile = columns // 2
    tile = per_tile * 2 * slice_rows
    tiles = patches // tile
    part_rows = slice_rows // 2
    sum_parts = [(flip, pl.ds(n * part_rows, part_rows)) for flip in (1, 0) for n in range(2)]

    def tile_at(n):
        return pl.ds(pl.multiple_of(n * tile, tile), tile)

    def own_send():
        links.send(("own_y", 0), rad, mine, partner)
        for by in others:
            links.send(("own_x", by), rad, mine, me_col[by])
        links.send(("own_s", 0), rad, mine, sibling)

    def reach_send(flip):
        for g, (first, count) in enumerate(parts):
            src = rad.at[pl.ds(0, count)]
            dst = grp.at[pl.ds(first, count), half]
            source_row = row_down(start_of(halves[flip]) + g)
            remote = links.copy(("grp", g, flip), src, dst, at(source_row, halves[flip], col, core))
            if g == 0 and flip == 0:
                near = local(src, dst)
                conditional.append(remote)
                win_copies.append(near)

                @pl.when(half == 1)
                def _(remote=remote):
                    remote.start()

                @pl.when(half == 0)
                def _(near=near):
                    near.start()
            else:
                remote.start()

    def opposite_send():
        for flip in range(2):
            target = at(row_down(rows // 2), halves[flip], col, core)
            links.send(("rf", 0), rad, rf.at[:, half, core], target, half)

    def far_send():
        for by in others:
            for side in range(2):
                src = far.at[:, :, far_columns(side, col_up(by))]
                links.send(("far", by, side), src, fbuf.at[side, :, col], me_col[by])

    def own_pass_y():
        piece = own.at[:, 1 - half, col, core]
        links.arrived(("own_y", 0), piece, partner)
        if split < nq:
            piece_b = own.at[b_part, 1 - half, col, core]
            for by in others:
                links.send(("own_xb", by), piece_b, piece_b, me_col[by])
        links.send(("own_sy", 0), piece, piece, sibling)

    def own_pass_x():
        for by in others:
            piece = own.at[:, half, col_down(by), core]
            links.arrived(("own_x", by), piece, me_col[by])
            if split:
                piece_a = own.at[a_part, half, col_down(by), core]
                links.send(("own_ya", by), piece_a, piece_a, partner)
            links.send(("own_sx", by), piece, piece, sibling)

    def own_end():
        for by in others:
            if split < nq:
                piece = own.at[b_part, 1 - half, col_down(by), core]
                links.arrived(("own_xb", by), piece, me_col[by])
                links.send(("own_sb", by), piece, piece, sibling)
            if split:
                piece = own.at[a_part, 1 - half, col_down(by), core]
                links.arrived(("own_ya", by), piece, partner)
                links.send(("own_sa", by), piece, piece, sibling)

    def reach_pass(flip):
        side = halves[flip]
        for g, (first, count) in enumerate(parts):
            piece = grp.at[pl.ds(first, count), side]
            if g == 0 and flip == 0:

                @pl.when(half == 1)
                def _(piece=piece):
                    links.arrived(("grp", 0, 0), piece, sibling)

                @pl.when(half == 0)
                def _():
                    win_copies[0].wait()
            else:
                links.arrived(("grp", g, flip), piece, sibling)
        for by in others:
            src = grp.at[pl.ds(2 * col_up(by), slots), side]
            links.send(("win_x", by, flip), src, win.at[:, side, col, core], me_col[by])
        made = local(grp.at[pl.ds(2 * col, slots), side], win.at[:, side, col, core])
        made.start()
        win_copies.append(made)
        if flip == 1:
            src = grp.at[pl.ds(2 * col + 1 - core, nq)]
            links.send(("win_s", 0), src, win.at[pl.ds(1 - core, nq), :, col, core], sibling)

    def mirror():
        own_copy.wait()
        links.arrived(("own_s", 0), own.at[:, half, col, 1 - core], sibling)
        links.arrived(("own_sy", 0), own.at[:, 1 - half, col, 1 - core], sibling)
        for by in others:
            src_col = col_down(by)
            links.arrived(("own_sx", by), own.at[:, half, src_col, 1 - core], sibling)
            if split:
                piece = own.at[a_part, 1 - half, src_col, 1 - core]
                links.arrived(("own_sa", by), piece, sibling)
            if split < nq:
                piece = own.at[b_part, 1 - half, src_col, 1 - core]
                links.arrived(("own_sb", by), piece, sibling)
        for q in range(nq):
            block_copies[q].wait()

            def mirrored(n, carry, q=q):
                product = lax.dot_general(
                    blocks[q, :, tile_at(n)],
                    own[q].reshape(patches, width),
                    (((0,), (0,)), ((), ())),
                    preferred_element_type=F32,
                )
                mr[q, n // 2, pl.ds((n % 2) * per_tile, per_tile)] = product.reshape(
                    per_tile, 2, slice_rows, width
                )
                return carry

            lax.fori_loop(0, tiles, mirrored, 0)
            links.send(("ms", q), mr.at[q, :, :, 1 - core], ms.at[q], sibling)

    def unite():
        for i in range(slots):
            if i < nq:
                links.arrived(("ms", i), ms.at[i], sibling)
            if i == 0:

                @pl.when(core == 0)
                def _():
                    un[0] = mr[0, :, :, 0]

                @pl.when(core == 1)
                def _():
                    un[0] = ms[0]
            elif i == nq:

                @pl.when(core == 0)
                def _():
                    un[nq] = ms[nq - 1]

                @pl.when(core == 1)
                def _():
                    un[nq] = mr[nq - 1, :, :, 1]
            else:
                un[i] = mr[i - core, :, :, core] + ms[i - 1 + core]

    def sums_send(part):
        flip, piece_rows = sum_parts[part]
        side = halves[flip]
        for by in others:
            src = un.at[:, side, col_up(by), piece_rows]
            links.send(("mx", by, part), src, mx.at[by - 1, :, side, piece_rows], me_col[by])

    def opposite_pass():
        for side in range(2):
            piece = rf.at[:, side, core]
            links.arrived(("rf", 0), piece, sibling, side)
            links.send(("rf_s", 0), piece, piece, sibling, side)

    def window_pass():
        for by in others:
            src_col = col_down(by)
            for flip in range(2):
                piece = win.at[:, halves[flip], src_col, core]
                links.arrived(("win_x", by, flip), piece, sibling)
            piece = win.at[pl.ds(1 - core, nq), :, src_col, core]
            links.send(("win_s", by), piece, piece, sibling)

    def forward():
        for made in win_copies[1:]:
            made.wait()
        for by in range(columns):
            piece = win.at[pl.ds(core, nq), :, col_down(by), 1 - core]
            links.arrived(("win_s", by), piece, sibling)
        for q in QORDER:

            def forwarded(n, carry, q=q):
                product = jnp.dot(
                    blocks[q, tile_at(n), :],
                    win[core + q].reshape(patches, width),
                    preferred_element_type=F32,
                )
                fw[q, n // 2, pl.ds((n % 2) * per_tile, per_tile)] = product.reshape(
                    per_tile, 2, slice_rows, width
                )
                return carry

            lax.fori_loop(0, tiles, forwarded, 0)
            links.send(("fs", q), fw.at[q, :, :, 1 - core], fs.at[q], sibling)

    def forward_unite(q):
        links.arrived(("fs", q), fs.at[q], sibling)
        fw[q, :, :, core] = fw[q, :, :, core] + fs[q]

        @pl.when((half == 0) & (2 * col <= q))
        def _():
            fw[q, :, :, core] = fw[q, :, :, core] + un[q - 2 * col]

        if q not in XFIRST:
            links.send(("fy", q), fw.at[q, 1 - half, :, core], fy.at[q], partner)

    def opposite(q):
        if q == QORDER[0]:
            for side in range(2):
                far_copies[side].wait()
                links.arrived(("rf_s", 0), rf.at[:, side, 1 - core], sibling, side)
                for by in others:
                    links.arrived(("far", by, side), fbuf.at[side, :, col_down(by)], sibling)
        depth = 2 * slice_rows
        product = sum(
            jnp.dot(
                fbuf[side, q].reshape(columns * slice_rows, depth),
                rf[q, side].reshape(depth, width),
                preferred_element_type=F32,
            )
            for side in range(2)
        )
        fw[q, half, :, core] = fw[q, half, :, core] + product.reshape(columns, slice_rows, width)
        if q in XFIRST:
            for by in others:
                links.send(("fx", by, q), fw.at[q, :, col_up(by), core], fx.at[by - 1, q], me_col[by])

    def forward_pass(q):
        if q in XFIRST:
            total = fw[q, :, col, core]
            for by in others:
                links.arrived(("fx", by, q), fx.at[by - 1, q], sibling)
                total = total + fx[by - 1, q]
            fw[q, :, col, core] = total
            links.send(("fy", q), fw.at[q, 1 - half, col, core], fy.at[q, 0], partner)
        else:
            links.arrived(("fy", q), fy.at[q], partner)
            fw[q, half, :, core] = fw[q, half, :, core] + fy[q]
            for by in others:
                links.send(
                    ("fx", by, q),
                    fw.at[q, half, col_up(by), core],
                    fx.at[by - 1, q, half],
                    me_col[by],
                )

    def forward_end(q):
        if q in XFIRST:
            links.arrived(("fy", q), fy.at[q, 0], partner)
            out[q] = fw[q, half, col, core] + fy[q, 0]
        else:
            total = fw[q, half, col, core]
            for by in others:
                links.arrived(("fx", by, q), fx.at[by - 1, q, half], sibling)
                total = total + fx[by - 1, q, half]
            out[q] = total

    def sums_pass(part):
        flip, piece_rows = sum_parts[part]
        side = halves[flip]
        hz_own[:, side, piece_rows] = jnp.zeros((groups, part_rows, width), F32)
        hz_own[pl.ds(2 * col, slots), side, piece_rows] = un[:, side, col, piece_rows]
        for by in others:
            links.arrived(("mx", by, part), mx.at[by - 1, :, side, piece_rows], sibling)
            reach = pl.ds(2 * col_down(by), slots)
            hz_own[reach, side, piece_rows] = (
                hz_own[reach, side, piece_rows] + mx[by - 1, :, side, piece_rows]
            )
        for g, (first, count) in enumerate(parts):
            src = hz_own.at[pl.ds(first, count), side, piece_rows]
            dst = hz.at[half, pl.ds(first, count), piece_rows]
            target = at(row_up(start_of(half) + g), side, col, core)
            remote = links.copy(("hz", g, part), src, dst, target)
            if g == 0:
                conditional.append(remote)

                @pl.when(half == 1)
                def _(remote=remote):
                    remote.start()
            else:
                remote.start()

    scope = locals()
    for step in ORDER:
        name, *args = step.split()
        scope[name](*map(int, args))

    kinds, bands = tab.shape
    reflect_of = jnp.concatenate([tab[...]] * (width // bands), axis=1)
    across = lax.broadcasted_iota(jnp.int32, (slice_rows, slice_rows), 1)
    down = lax.broadcasted_iota(jnp.int32, (slice_rows, slice_rows), 0)

    def upright(values):
        spread = jnp.broadcast_to(values, (slice_rows, slice_rows))
        return jnp.sum(jnp.where(across == down, spread, 0), axis=1, keepdims=True)

    for q in range(nq):
        kind = upright(mat[pl.ds(q, 1), :])
        reflect = jnp.zeros((slice_rows, width), F32)
        for m in range(kinds):
            reflect = jnp.where(kind == m, reflect_of[m : m + 1, :], reflect)
        refl[q] = reflect
    emi_copy.wait()
    for q in range(nq):
        forward_end(q)
    for part, (flip, piece_rows) in enumerate(sum_parts):
        for g, (first, count) in enumerate(parts):
            piece = hz.at[halves[flip], pl.ds(first, count), piece_rows]
            if g == 0:

                @pl.when(halves[flip] == 1)
                def _(piece=piece, part=part):
                    links.arrived(("hz", 0, part), piece, sibling)
            else:
                links.arrived(("hz", g, part), piece, sibling)
    for q in range(nq):
        total = out[q]
        for half_from in range(2):
            for u in range(q + (0 if half_from else nq), groups, nq):
                total = total + hz[half_from, u]
        irradiation = total / upright(area[pl.ds(q, 1), :])
        out[q] = emi_v[q].astype(F32) + refl[q] * irradiation

    for made in links.sent:
        if any(made is other for other in conditional):

            @pl.when(half == 1)
            def _(made=made):
                made.wait_send()
        else:
            made.wait_send()


def on_device(rows, columns, radiosity, emission, areas, patch_material, reflect_table, pair_blocks, far_blocks):
    nq, slice_rows, width = radiosity.shape
    patches = pair_blocks.shape[2]
    slots = nq + 1
    groups = 2 * columns + nq - 1
    bf16 = jnp.bfloat16
    scratch = [
        pltpu.VMEM((nq, patches, patches), bf16),
        pltpu.VMEM((nq, 2, columns, 2, slice_rows, width), bf16),
        pltpu.VMEM((slots, 2, columns, 2, slice_rows, width), bf16),
        pltpu.VMEM((groups, 2, slice_rows, width), bf16),
        pltpu.VMEM((2, nq, columns, slice_rows, 2 * slice_rows), bf16),
        pltpu.VMEM((nq, 2, 2, slice_rows, width), bf16),
        pltpu.VMEM((nq, 2, columns, 2, slice_rows, width), F32),
        pltpu.VMEM((nq, 2, columns, slice_rows, width), F32),
        pltpu.VMEM((nq, columns, slice_rows, width), F32),
        pltpu.VMEM((columns - 1, nq, 2, slice_rows, width), F32),
        pltpu.VMEM((nq, 2, columns, 2, slice_rows, width), F32),
        pltpu.VMEM((nq, 2, columns, slice_rows, width), F32),
        pltpu.VMEM((slots, 2, columns, slice_rows, width), F32),
        pltpu.VMEM((columns - 1, slots, 2, slice_rows, width), F32),
        pltpu.VMEM((groups, 2, slice_rows, width), F32),
        pltpu.VMEM((2, groups, slice_rows, width), F32),
        pltpu.VMEM((nq, slice_rows, width), bf16),
        pltpu.VMEM((nq, slice_rows, width), F32),
        pltpu.SemaphoreType.DMA((160,)),
        pltpu.SemaphoreType.DMA((160,)),
        pltpu.SemaphoreType.DMA((16,)),
    ]
    any_space = pl.BlockSpec(memory_space=pl.ANY)
    vmem = pl.BlockSpec(memory_space=pltpu.VMEM)
    flops = 4 * nq * patches * patches * width
    return pl.pallas_call(
        functools.partial(kernel, rows, columns),
        out_shape=jax.ShapeDtypeStruct((nq, slice_rows, width), F32),
        in_specs=[any_space, any_space, vmem, vmem, vmem, any_space, any_space],
        out_specs=vmem,
        scratch_shapes=scratch,
        compiler_params=pltpu.CompilerParams(
            collective_id=0, has_side_effects=True, vmem_limit_bytes=58 * 2**20
        ),
        cost_estimate=pl.CostEstimate(
            flops=flops, bytes_accessed=2 * nq * patches * patches, transcendentals=0
        ),
    )(radiosity, emission, areas, patch_material, reflect_table, pair_blocks, far_blocks)


def solution(mesh):
    rows, stops = mesh.shape["row"], mesh.shape["stop"]
    return jax.shard_map(
        functools.partial(on_device, rows, stops // 4),
        mesh=mesh,
        in_specs=(
            P("row", "stop", None),
            P("row", "stop", None),
            P("row", "stop"),
            P("row", "stop"),
            P(),
            P("row", "stop", None, None),
            P("row", "stop", None),
        ),
        out_specs=P("row", "stop", None),
        check_vma=False,
    )
```

```python
import functools

import jax
import jax.numpy as jnp
from jax import lax
from jax.experimental import pallas as pl
from jax.experimental.pallas import tpu as pltpu
from jax.sharding import PartitionSpec as P

MESH = pl.DeviceIdType.MESH
F32 = jnp.float32


SPLIT = 0
XFIRST = ()
QORDER = (0, 1, 2, 3)
ORDER = (
    "own_send",
    "reach_send 0",
    "reach_send 1",
    "reach_send 2",
    "reach_send 3",
    "own_pass_y",
    "own_pass_x",
    "reach_pass 0",
    "reach_pass 1",
    "own_end",
    "reach_pass 2",
    "mirror",
    "reach_pass 3",
    "opposite_send",
    "unite",
    "opposite_pass",
    "window_pass",
    "sums_send 0",
    "sums_send 1",
    "far_send",
    "sums_send 2",
    "sums_send 3",
    "forward",
    "forward_unite 0",
    "forward_unite 1",
    "forward_unite 2",
    "forward_unite 3",
    "opposite 0",
    "opposite 1",
    "opposite 2",
    "opposite 3",
    "sums_pass 0",
    "forward_pass 0",
    "sums_pass 1",
    "forward_pass 1",
    "sums_pass 2",
    "forward_pass 2",
    "sums_pass 3",
    "forward_pass 3",
)


class Links:
    def __init__(self, send_sem, recv_sem):
        self.send_sem, self.recv_sem = send_sem, recv_sem
        self.names, self.recv_count, self.sent = {}, 0, []

    def name(self, key, count=1):
        self.names[key] = self.recv_count
        self.recv_count += count

    def copy(self, key, src, dst, target, extra=0):
        made = pltpu.make_async_remote_copy(
            src_ref=src,
            dst_ref=dst,
            send_sem=self.send_sem.at[len(self.sent)],
            recv_sem=self.recv_sem.at[self.names[key] + extra],
            device_id=target,
            device_id_type=MESH,
        )
        self.sent.append(made)
        return made

    def send(self, key, src, dst, target, extra=0):
        self.copy(key, src, dst, target, extra).start()

    def arrived(self, key, dst, target, extra=0):
        pltpu.make_async_remote_copy(
            src_ref=dst,
            dst_ref=dst,
            send_sem=self.send_sem.at[0],
            recv_sem=self.recv_sem.at[self.names[key] + extra],
            device_id=target,
            device_id_type=MESH,
        ).wait_recv()


def kernel(
    rows, columns,
    rad, emi, area, mat, tab, pair, far, out,
    blocks, own, win, grp, fbuf, rf, fw, fs, fy, fx, mr, ms, un, mx, hz_own, hz, emi_v, refl,
    send_sem, recv_sem, local_sem,
):
    nq, slice_rows, width = rad.shape
    patches = pair.shape[2]
    half_patches = patches // 2
    slots = nq + 1
    groups = 2 * columns + nq - 1
    parts = [(g * nq, min(nq, groups - g * nq)) for g in range(-(-groups // nq))]
    row, stop = lax.axis_index("row"), lax.axis_index("stop")
    half, col, core = stop // (2 * columns), (stop // 2) % columns, stop % 2
    others = range(1, columns)

    def at(row_by, half_to, col_to, core_to):
        return (row_by, half_to * (2 * columns) + col_to * 2 + core_to)

    def row_up(by):
        return lax.rem(row + by, rows)

    def row_down(by):
        return lax.rem(row + rows - by, rows)

    def col_up(by):
        return lax.rem(col + by, columns)

    def col_down(by):
        return lax.rem(col + columns - by, columns)

    sibling = at(row, half, col, 1 - core)
    partner = at(row, 1 - half, col, core)
    me_col = {by: at(row, half, col_up(by), core) for by in others}
    starts = (0, 2 * columns // nq)
    halves = (half, 1 - half)

    def start_of(which):
        return jnp.where(which == 0, starts[0], starts[1])

    split = SPLIT
    links = Links(send_sem, recv_sem)
    for by in others:
        for key in ("own_x", "own_sx", "own_ya", "own_xb", "own_sa", "own_sb"):
            links.name((key, by))
        for side in range(2):
            links.name(("far", by, side))
        for part in range(4):
            links.name(("mx", by, part))
            links.name(("win_x", by, part))
        for q in range(nq):
            links.name(("fx", by, q))
    for by in range(columns):
        links.name(("win_s", by))
    for key in ("own_s", "own_y", "own_sy"):
        links.name((key, 0))
    for key in ("rf", "rf_s"):
        links.name((key, 0), 2)
    for g in range(len(parts)):
        for part in range(4):
            links.name(("hz", g, part))
            links.name(("grp", g, part))
    for q in range(nq):
        for key in ("ms", "fs", "fy"):
            links.name((key, q))

    local_count = [0]

    def local(src, dst):
        made = pltpu.make_async_copy(src, dst, local_sem.at[local_count[0]])
        local_count[0] += 1
        return made

    def far_columns(side, column):
        first = side * half_patches + column * (2 * slice_rows)
        return pl.ds(pl.multiple_of(first, 2 * slice_rows), 2 * slice_rows)

    def offsets(mine, theirs):
        reach = {starts[mine] + g for g in range(len(parts))}
        back = {-(starts[theirs] + g) for g in range(len(parts))}
        both = {by % rows for by in reach | back | {rows // 2}}
        return sorted(both - {0} if mine == theirs else both)

    barrier = pltpu.get_barrier_semaphore()
    peers = []
    for a, b in zip(offsets(0, 1), offsets(1, 0), strict=True):
        peers.append(at(row_up(jnp.where(half == 0, a, b)), 1 - half, col, core))
    for a, b in zip(offsets(0, 0), offsets(1, 1), strict=True):
        peers.append(at(row_up(jnp.where(half == 0, a, b)), half, col, core))
    peers += [me_col[by] for by in others] + [sibling]
    for peer in peers:
        pl.semaphore_signal(barrier, inc=1, device_id=peer, device_id_type=MESH)

    own_copy = local(rad, own.at[:, half, col, core])
    own_copy.start()
    block_copies = []
    for q in range(nq):
        made = local(pair.at[q, 0], blocks.at[q])
        made.start()
        block_copies.append(made)
    far_copies = []
    for side in range(2):
        made = local(far.at[:, :, far_columns(side, col)], fbuf.at[side, :, col])
        made.start()
        far_copies.append(made)
    emi_copy = local(emi, emi_v)
    emi_copy.start()
    pl.semaphore_wait(barrier, len(peers))

    mine = own.at[:, half, col, core]
    win_copies, near_copies, conditional = [], [], []
    a_part, b_part = pl.ds(0, split), pl.ds(split, nq - split)
    per_tile = columns
    tile = per_tile * 2 * slice_rows
    tiles = patches // tile
    part_rows = slice_rows // 2
    row_parts = [pl.ds(n * part_rows, part_rows) for n in range(2)]
    sum_parts = [(flip, piece_rows) for flip in (1, 0) for piece_rows in row_parts]
    reach_parts = [(flip, piece_rows) for flip in (0, 1) for piece_rows in row_parts]

    def tile_at(n):
        return pl.ds(pl.multiple_of(n * tile, tile), tile)

    def own_send():
        links.send(("own_y", 0), rad, mine, partner)
        for by in others:
            links.send(("own_x", by), rad, mine, me_col[by])
        links.send(("own_s", 0), rad, mine, sibling)

    def reach_send(part):
        flip, piece_rows = reach_parts[part]
        for g, (first, count) in enumerate(parts):
            src = rad.at[pl.ds(0, count), piece_rows]
            dst = grp.at[pl.ds(first, count), half, piece_rows]
            source_row = row_down(start_of(halves[flip]) + g)
            target = at(source_row, halves[flip], col, core)
            remote = links.copy(("grp", g, part), src, dst, target)
            if g == 0 and flip == 0:
                near = local(src, dst)
                conditional.append(remote)
                near_copies.append(near)

                @pl.when(half == 1)
                def _(remote=remote):
                    remote.start()

                @pl.when(half == 0)
                def _(near=near):
                    near.start()
            else:
                remote.start()

    def opposite_send():
        for flip in range(2):
            target = at(row_down(rows // 2), halves[flip], col, core)
            links.send(("rf", 0), rad, rf.at[:, half, core], target, half)

    def far_send():
        for by in others:
            for side in range(2):
                src = far.at[:, :, far_columns(side, col_up(by))]
                links.send(("far", by, side), src, fbuf.at[side, :, col], me_col[by])

    def own_pass_y():
        piece = own.at[:, 1 - half, col, core]
        links.arrived(("own_y", 0), piece, partner)
        if split < nq:
            piece_b = own.at[b_part, 1 - half, col, core]
            for by in others:
                links.send(("own_xb", by), piece_b, piece_b, me_col[by])
        links.send(("own_sy", 0), piece, piece, sibling)

    def own_pass_x():
        for by in others:
            piece = own.at[:, half, col_down(by), core]
            links.arrived(("own_x", by), piece, me_col[by])
            if split:
                piece_a = own.at[a_part, half, col_down(by), core]
                links.send(("own_ya", by), piece_a, piece_a, partner)
            links.send(("own_sx", by), piece, piece, sibling)

    def own_end():
        for by in others:
            if split < nq:
                piece = own.at[b_part, 1 - half, col_down(by), core]
                links.arrived(("own_xb", by), piece, me_col[by])
                links.send(("own_sb", by), piece, piece, sibling)
            if split:
                piece = own.at[a_part, 1 - half, col_down(by), core]
                links.arrived(("own_ya", by), piece, partner)
                links.send(("own_sa", by), piece, piece, sibling)

    def reach_pass(part):
        flip, piece_rows = reach_parts[part]
        side = halves[flip]
        for g, (first, count) in enumerate(parts):
            piece = grp.at[pl.ds(first, count), side, piece_rows]
            if g == 0 and flip == 0:
                near = near_copies[part]

                @pl.when(half == 1)
                def _(piece=piece):
                    links.arrived(("grp", 0, part), piece, sibling)

                @pl.when(half == 0)
                def _():
                    near.wait()
            else:
                links.arrived(("grp", g, part), piece, sibling)
        dst = win.at[:, side, col, core, piece_rows]
        for by in others:
            src = grp.at[pl.ds(2 * col_up(by), slots), side, piece_rows]
            links.send(("win_x", by, part), src, dst, me_col[by])
        made = local(grp.at[pl.ds(2 * col, slots), side, piece_rows], dst)
        made.start()
        win_copies.append(made)
        if part == 3:
            src = grp.at[pl.ds(2 * col + 1 - core, nq)]
            links.send(("win_s", 0), src, win.at[pl.ds(1 - core, nq), :, col, core], sibling)

    def mirror():
        own_copy.wait()
        links.arrived(("own_s", 0), own.at[:, half, col, 1 - core], sibling)
        links.arrived(("own_sy", 0), own.at[:, 1 - half, col, 1 - core], sibling)
        for by in others:
            src_col = col_down(by)
            links.arrived(("own_sx", by), own.at[:, half, src_col, 1 - core], sibling)
            if split:
                piece = own.at[a_part, 1 - half, src_col, 1 - core]
                links.arrived(("own_sa", by), piece, sibling)
            if split < nq:
                piece = own.at[b_part, 1 - half, src_col, 1 - core]
                links.arrived(("own_sb", by), piece, sibling)
        for q in range(nq):
            block_copies[q].wait()

            def mirrored(n, carry, q=q):
                product = lax.dot_general(
                    blocks[q, :, tile_at(n)],
                    own[q].reshape(patches, width),
                    (((0,), (0,)), ((), ())),
                    preferred_element_type=F32,
                )
                mr[q, n] = product.reshape(
                    per_tile, 2, slice_rows, width
                )
                return carry

            lax.fori_loop(0, tiles, mirrored, 0, unroll=True)
            links.send(("ms", q), mr.at[q, :, :, 1 - core], ms.at[q], sibling)

    def unite():
        for i in range(slots):
            if i < nq:
                links.arrived(("ms", i), ms.at[i], sibling)
            if i == 0:

                @pl.when(core == 0)
                def _():
                    un[0] = mr[0, :, :, 0]

                @pl.when(core == 1)
                def _():
                    un[0] = ms[0]
            elif i == nq:

                @pl.when(core == 0)
                def _():
                    un[nq] = ms[nq - 1]

                @pl.when(core == 1)
                def _():
                    un[nq] = mr[nq - 1, :, :, 1]
            else:
                un[i] = mr[i - core, :, :, core] + ms[i - 1 + core]

    def sums_send(part):
        flip, piece_rows = sum_parts[part]
        side = halves[flip]
        for by in others:
            src = un.at[:, side, col_up(by), piece_rows]
            links.send(("mx", by, part), src, mx.at[by - 1, :, side, piece_rows], me_col[by])

    def opposite_pass():
        for side in range(2):
            piece = rf.at[:, side, core]
            links.arrived(("rf", 0), piece, sibling, side)
            links.send(("rf_s", 0), piece, piece, sibling, side)

    def window_pass():
        for by in others:
            src_col = col_down(by)
            for part, (flip, piece_rows) in enumerate(reach_parts):
                piece = win.at[:, halves[flip], src_col, core, piece_rows]
                links.arrived(("win_x", by, part), piece, sibling)
            piece = win.at[pl.ds(1 - core, nq), :, src_col, core]
            links.send(("win_s", by), piece, piece, sibling)

    def forward():
        for made in win_copies:
            made.wait()
        for by in range(columns):
            piece = win.at[pl.ds(core, nq), :, col_down(by), 1 - core]
            links.arrived(("win_s", by), piece, sibling)
        for q in QORDER:

            def forwarded(n, carry, q=q):
                product = jnp.dot(
                    blocks[q, tile_at(n), :],
                    win[core + q].reshape(patches, width),
                    preferred_element_type=F32,
                )
                fw[q, n] = product.reshape(
                    per_tile, 2, slice_rows, width
                )
                return carry

            lax.fori_loop(0, tiles, forwarded, 0, unroll=True)
            links.send(("fs", q), fw.at[q, :, :, 1 - core], fs.at[q], sibling)

    def forward_unite(q):
        links.arrived(("fs", q), fs.at[q], sibling)
        fw[q, :, :, core] = fw[q, :, :, core] + fs[q]

        @pl.when((half == 0) & (2 * col <= q))
        def _():
            fw[q, :, :, core] = fw[q, :, :, core] + un[q - 2 * col]

        if q not in XFIRST:
            links.send(("fy", q), fw.at[q, 1 - half, :, core], fy.at[q], partner)

    def opposite(q):
        if q == QORDER[0]:
            for side in range(2):
                far_copies[side].wait()
                links.arrived(("rf_s", 0), rf.at[:, side, 1 - core], sibling, side)
                for by in others:
                    links.arrived(("far", by, side), fbuf.at[side, :, col_down(by)], sibling)
        depth = 2 * slice_rows
        product = sum(
            jnp.dot(
                fbuf[side, q].reshape(columns * slice_rows, depth),
                rf[q, side].reshape(depth, width),
                preferred_element_type=F32,
            )
            for side in range(2)
        )
        fw[q, half, :, core] = fw[q, half, :, core] + product.reshape(columns, slice_rows, width)
        if q in XFIRST:
            for by in others:
                links.send(("fx", by, q), fw.at[q, :, col_up(by), core], fx.at[by - 1, q], me_col[by])

    def forward_pass(q):
        if q in XFIRST:
            total = fw[q, :, col, core]
            for by in others:
                links.arrived(("fx", by, q), fx.at[by - 1, q], sibling)
                total = total + fx[by - 1, q]
            fw[q, :, col, core] = total
            links.send(("fy", q), fw.at[q, 1 - half, col, core], fy.at[q, 0], partner)
        else:
            links.arrived(("fy", q), fy.at[q], partner)
            fw[q, half, :, core] = fw[q, half, :, core] + fy[q]
            for by in others:
                links.send(
                    ("fx", by, q),
                    fw.at[q, half, col_up(by), core],
                    fx.at[by - 1, q, half],
                    me_col[by],
                )

    def forward_end(q):
        if q in XFIRST:
            links.arrived(("fy", q), fy.at[q, 0], partner)
            out[q] = fw[q, half, col, core] + fy[q, 0]
        else:
            total = fw[q, half, col, core]
            for by in others:
                links.arrived(("fx", by, q), fx.at[by - 1, q, half], sibling)
                total = total + fx[by - 1, q, half]
            out[q] = total

    def sums_pass(part):
        flip, piece_rows = sum_parts[part]
        side = halves[flip]
        hz_own[:, side, piece_rows] = jnp.zeros((groups, part_rows, width), F32)
        hz_own[pl.ds(2 * col, slots), side, piece_rows] = un[:, side, col, piece_rows]
        for by in others:
            links.arrived(("mx", by, part), mx.at[by - 1, :, side, piece_rows], sibling)
            reach = pl.ds(2 * col_down(by), slots)
            hz_own[reach, side, piece_rows] = (
                hz_own[reach, side, piece_rows] + mx[by - 1, :, side, piece_rows]
            )
        for g, (first, count) in enumerate(parts):
            src = hz_own.at[pl.ds(first, count), side, piece_rows]
            dst = hz.at[half, pl.ds(first, count), piece_rows]
            target = at(row_up(start_of(half) + g), side, col, core)
            remote = links.copy(("hz", g, part), src, dst, target)
            if g == 0:
                conditional.append(remote)

                @pl.when(half == 1)
                def _(remote=remote):
                    remote.start()
            else:
                remote.start()

    scope = locals()
    for step in ORDER:
        name, *args = step.split()
        scope[name](*map(int, args))

    kinds, bands = tab.shape
    reflect_of = jnp.concatenate([tab[...]] * (width // bands), axis=1)
    across = lax.broadcasted_iota(jnp.int32, (slice_rows, slice_rows), 1)
    down = lax.broadcasted_iota(jnp.int32, (slice_rows, slice_rows), 0)

    def upright(values):
        spread = jnp.broadcast_to(values, (slice_rows, slice_rows))
        return jnp.sum(jnp.where(across == down, spread, 0), axis=1, keepdims=True)

    for q in range(nq):
        kind = upright(mat[pl.ds(q, 1), :])
        reflect = jnp.zeros((slice_rows, width), F32)
        for m in range(kinds):
            reflect = jnp.where(kind == m, reflect_of[m : m + 1, :], reflect)
        refl[q] = reflect
    emi_copy.wait()
    for q in range(nq):
        forward_end(q)
    for part, (flip, piece_rows) in enumerate(sum_parts):
        for g, (first, count) in enumerate(parts):
            piece = hz.at[halves[flip], pl.ds(first, count), piece_rows]
            if g == 0:

                @pl.when(halves[flip] == 1)
                def _(piece=piece, part=part):
                    links.arrived(("hz", 0, part), piece, sibling)
            else:
                links.arrived(("hz", g, part), piece, sibling)
    for q in range(nq):
        total = out[q]
        for half_from in range(2):
            for u in range(q + (0 if half_from else nq), groups, nq):
                total = total + hz[half_from, u]
        irradiation = total / upright(area[pl.ds(q, 1), :])
        out[q] = emi_v[q].astype(F32) + refl[q] * irradiation

    for made in links.sent:
        if any(made is other for other in conditional):

            @pl.when(half == 1)
            def _(made=made):
                made.wait_send()
        else:
            made.wait_send()


def on_device(rows, columns, radiosity, emission, areas, patch_material, reflect_table, pair_blocks, far_blocks):
    nq, slice_rows, width = radiosity.shape
    patches = pair_blocks.shape[2]
    slots = nq + 1
    groups = 2 * columns + nq - 1
    bf16 = jnp.bfloat16
    scratch = [
        pltpu.VMEM((nq, patches, patches), bf16),
        pltpu.VMEM((nq, 2, columns, 2, slice_rows, width), bf16),
        pltpu.VMEM((slots, 2, columns, 2, slice_rows, width), bf16),
        pltpu.VMEM((groups, 2, slice_rows, width), bf16),
        pltpu.VMEM((2, nq, columns, slice_rows, 2 * slice_rows), bf16),
        pltpu.VMEM((nq, 2, 2, slice_rows, width), bf16),
        pltpu.VMEM((nq, 2, columns, 2, slice_rows, width), F32),
        pltpu.VMEM((nq, 2, columns, slice_rows, width), F32),
        pltpu.VMEM((nq, columns, slice_rows, width), F32),
        pltpu.VMEM((columns - 1, nq, 2, slice_rows, width), F32),
        pltpu.VMEM((nq, 2, columns, 2, slice_rows, width), F32),
        pltpu.VMEM((nq, 2, columns, slice_rows, width), F32),
        pltpu.VMEM((slots, 2, columns, slice_rows, width), F32),
        pltpu.VMEM((columns - 1, slots, 2, slice_rows, width), F32),
        pltpu.VMEM((groups, 2, slice_rows, width), F32),
        pltpu.VMEM((2, groups, slice_rows, width), F32),
        pltpu.VMEM((nq, slice_rows, width), bf16),
        pltpu.VMEM((nq, slice_rows, width), F32),
        pltpu.SemaphoreType.DMA((160,)),
        pltpu.SemaphoreType.DMA((160,)),
        pltpu.SemaphoreType.DMA((24,)),
    ]
    any_space = pl.BlockSpec(memory_space=pl.ANY)
    vmem = pl.BlockSpec(memory_space=pltpu.VMEM)
    flops = 4 * nq * patches * patches * width
    return pl.pallas_call(
        functools.partial(kernel, rows, columns),
        out_shape=jax.ShapeDtypeStruct((nq, slice_rows, width), F32),
        in_specs=[any_space, any_space, vmem, vmem, vmem, any_space, any_space],
        out_specs=vmem,
        scratch_shapes=scratch,
        compiler_params=pltpu.CompilerParams(
            collective_id=0, has_side_effects=True, vmem_limit_bytes=58 * 2**20
        ),
        cost_estimate=pl.CostEstimate(
            flops=flops, bytes_accessed=2 * nq * patches * patches, transcendentals=0
        ),
    )(radiosity, emission, areas, patch_material, reflect_table, pair_blocks, far_blocks)


def solution(mesh):
    rows, stops = mesh.shape["row"], mesh.shape["stop"]
    return jax.shard_map(
        functools.partial(on_device, rows, stops // 4),
        mesh=mesh,
        in_specs=(
            P("row", "stop", None),
            P("row", "stop", None),
            P("row", "stop"),
            P("row", "stop"),
            P(),
            P("row", "stop", None, None),
            P("row", "stop", None),
        ),
        out_specs=P("row", "stop", None),
        check_vma=False,
    )
```

```python
import functools

import jax
import jax.numpy as jnp
from jax import lax
from jax.experimental import pallas as pl
from jax.experimental.pallas import tpu as pltpu
from jax.sharding import PartitionSpec as P

MESH = pl.DeviceIdType.MESH
F32 = jnp.float32


SPLIT = 0
XFIRST = ()
ORDER = (
    "own_send",
    "reach_send 0",
    "reach_send 1",
    "reach_send 2",
    "reach_send 3",
    "own_pass_y",
    "own_pass_x",
    "reach_pass 0",
    "reach_pass 1",
    "own_end",
    "reach_pass 2",
    "mirror",
    "reach_pass 3",
    "opposite_send",
    "unite",
    "opposite_pass",
    "window_pass",
    "sums_send 0",
    "sums_send 1",
    "far_send",
    "sums_send 2",
    "forward 0",
    "forward 1",
    "forward_unite 0",
    "forward 2",
    "forward_unite 1",
    "forward 3",
    "forward_unite 2",
    "forward_unite 3",
    "opposite 0",
    "opposite 1",
    "opposite 2",
    "opposite 3",
    "sums_pass 0",
    "sums_send 3",
    "forward_pass 0",
    "sums_pass 1",
    "forward_pass 1",
    "sums_pass 2",
    "forward_pass 2",
    "sums_pass 3",
    "forward_pass 3",
)


class Links:
    def __init__(self, send_sem, recv_sem):
        self.send_sem, self.recv_sem = send_sem, recv_sem
        self.names, self.recv_count, self.sent = {}, 0, []

    def name(self, key, count=1):
        self.names[key] = self.recv_count
        self.recv_count += count

    def copy(self, key, src, dst, target, extra=0):
        made = pltpu.make_async_remote_copy(
            src_ref=src,
            dst_ref=dst,
            send_sem=self.send_sem.at[len(self.sent)],
            recv_sem=self.recv_sem.at[self.names[key] + extra],
            device_id=target,
            device_id_type=MESH,
        )
        self.sent.append(made)
        return made

    def send(self, key, src, dst, target, extra=0):
        self.copy(key, src, dst, target, extra).start()

    def arrived(self, key, dst, target, extra=0):
        pltpu.make_async_remote_copy(
            src_ref=dst,
            dst_ref=dst,
            send_sem=self.send_sem.at[0],
            recv_sem=self.recv_sem.at[self.names[key] + extra],
            device_id=target,
            device_id_type=MESH,
        ).wait_recv()


def kernel(
    rows, columns,
    rad, emi, area_in, mat_in, tab_in, pair, far, result,
    blocks, own, win, grp, fbuf, rf, fw, fs, fy, fx, mr, ms, un, mx, hz_own, hz, emi_v, refl,
    area, mat, tab, out,
    send_sem, recv_sem, local_sem,
):
    nq, slice_rows, width = rad.shape
    patches = pair.shape[2]
    half_patches = patches // 2
    slots = nq + 1
    groups = 2 * columns + nq - 1
    parts = [(g * nq, min(nq, groups - g * nq)) for g in range(-(-groups // nq))]
    row, stop = lax.axis_index("row"), lax.axis_index("stop")
    half, col, core = stop // (2 * columns), (stop // 2) % columns, stop % 2
    others = range(1, columns)

    def at(row_by, half_to, col_to, core_to):
        return (row_by, half_to * (2 * columns) + col_to * 2 + core_to)

    def row_up(by):
        return lax.rem(row + by, rows)

    def row_down(by):
        return lax.rem(row + rows - by, rows)

    def col_up(by):
        return lax.rem(col + by, columns)

    def col_down(by):
        return lax.rem(col + columns - by, columns)

    sibling = at(row, half, col, 1 - core)
    partner = at(row, 1 - half, col, core)
    me_col = {by: at(row, half, col_up(by), core) for by in others}
    starts = (0, 2 * columns // nq)
    halves = (half, 1 - half)

    def start_of(which):
        return jnp.where(which == 0, starts[0], starts[1])

    split = SPLIT
    links = Links(send_sem, recv_sem)
    for by in others:
        for key in ("own_x", "own_sx", "own_ya", "own_xb", "own_sa", "own_sb"):
            links.name((key, by))
        for side in range(2):
            links.name(("far", by, side))
        for part in range(4):
            links.name(("mx", by, part))
            links.name(("win_x", by, part))
        for q in range(nq):
            links.name(("fx", by, q))
    for by in range(columns):
        links.name(("win_s", by))
    for key in ("own_s", "own_y", "own_sy"):
        links.name((key, 0))
    for key in ("rf", "rf_s"):
        links.name((key, 0), 2)
    for g in range(len(parts)):
        for part in range(4):
            links.name(("hz", g, part))
            links.name(("grp", g, part))
    for q in range(nq):
        for key in ("ms", "fs", "fy"):
            links.name((key, q))

    local_count = [0]

    def local(src, dst):
        made = pltpu.make_async_copy(src, dst, local_sem.at[local_count[0]])
        local_count[0] += 1
        return made

    def far_columns(side, column):
        first = side * half_patches + column * (2 * slice_rows)
        return pl.ds(pl.multiple_of(first, 2 * slice_rows), 2 * slice_rows)

    def offsets(mine, theirs):
        reach = {starts[mine] + g for g in range(len(parts))}
        back = {-(starts[theirs] + g) for g in range(len(parts))}
        both = {by % rows for by in reach | back | {rows // 2}}
        return sorted(both - {0} if mine == theirs else both)

    barrier = pltpu.get_barrier_semaphore()
    peers = []
    for a, b in zip(offsets(0, 1), offsets(1, 0), strict=True):
        peers.append(at(row_up(jnp.where(half == 0, a, b)), 1 - half, col, core))
    for a, b in zip(offsets(0, 0), offsets(1, 1), strict=True):
        peers.append(at(row_up(jnp.where(half == 0, a, b)), half, col, core))
    peers += [me_col[by] for by in others] + [sibling]
    for peer in peers:
        pl.semaphore_signal(barrier, inc=1, device_id=peer, device_id_type=MESH)

    own_copy = local(rad, own.at[:, half, col, core])
    own_copy.start()
    block_copies = []
    for q in range(nq):
        made = local(pair.at[q, 0], blocks.at[q])
        made.start()
        block_copies.append(made)
    far_copies = []
    for side in range(2):
        made = local(far.at[:, :, far_columns(side, col)], fbuf.at[side, :, col])
        made.start()
        far_copies.append(made)
    small_copies = []
    for src, dst in ((emi, emi_v), (area_in, area), (mat_in, mat), (tab_in, tab)):
        made = local(src, dst)
        made.start()
        small_copies.append(made)
    pl.semaphore_wait(barrier, len(peers))

    mine = own.at[:, half, col, core]
    win_copies, near_copies, conditional = [], [], []
    a_part, b_part = pl.ds(0, split), pl.ds(split, nq - split)
    per_tile = columns
    tile = per_tile * 2 * slice_rows
    tiles = patches // tile
    part_rows = slice_rows // 2
    row_parts = [pl.ds(n * part_rows, part_rows) for n in range(2)]
    sum_parts = [(flip, piece_rows) for flip in (1, 0) for piece_rows in row_parts]
    reach_parts = [(flip, piece_rows) for flip in (0, 1) for piece_rows in row_parts]

    def tile_at(n):
        return pl.ds(pl.multiple_of(n * tile, tile), tile)

    def own_send():
        links.send(("own_y", 0), rad, mine, partner)
        for by in others:
            links.send(("own_x", by), rad, mine, me_col[by])
        links.send(("own_s", 0), rad, mine, sibling)

    def reach_send(part):
        flip, piece_rows = reach_parts[part]
        for g, (first, count) in enumerate(parts):
            src = rad.at[pl.ds(0, count), piece_rows]
            dst = grp.at[pl.ds(first, count), half, piece_rows]
            source_row = row_down(start_of(halves[flip]) + g)
            target = at(source_row, halves[flip], col, core)
            remote = links.copy(("grp", g, part), src, dst, target)
            if g == 0 and flip == 0:
                near = local(src, dst)
                conditional.append(remote)
                near_copies.append(near)

                @pl.when(half == 1)
                def _(remote=remote):
                    remote.start()

                @pl.when(half == 0)
                def _(near=near):
                    near.start()
            else:
                remote.start()

    def opposite_send():
        for flip in range(2):
            target = at(row_down(rows // 2), halves[flip], col, core)
            links.send(("rf", 0), rad, rf.at[:, half, core], target, half)

    def far_send():
        for by in others:
            for side in range(2):
                src = far.at[:, :, far_columns(side, col_up(by))]
                links.send(("far", by, side), src, fbuf.at[side, :, col], me_col[by])

    def own_pass_y():
        piece = own.at[:, 1 - half, col, core]
        links.arrived(("own_y", 0), piece, partner)
        if split < nq:
            piece_b = own.at[b_part, 1 - half, col, core]
            for by in others:
                links.send(("own_xb", by), piece_b, piece_b, me_col[by])
        links.send(("own_sy", 0), piece, piece, sibling)

    def own_pass_x():
        for by in others:
            piece = own.at[:, half, col_down(by), core]
            links.arrived(("own_x", by), piece, me_col[by])
            if split:
                piece_a = own.at[a_part, half, col_down(by), core]
                links.send(("own_ya", by), piece_a, piece_a, partner)
            links.send(("own_sx", by), piece, piece, sibling)

    def own_end():
        for by in others:
            if split < nq:
                piece = own.at[b_part, 1 - half, col_down(by), core]
                links.arrived(("own_xb", by), piece, me_col[by])
                links.send(("own_sb", by), piece, piece, sibling)
            if split:
                piece = own.at[a_part, 1 - half, col_down(by), core]
                links.arrived(("own_ya", by), piece, partner)
                links.send(("own_sa", by), piece, piece, sibling)

    def reach_pass(part):
        flip, piece_rows = reach_parts[part]
        side = halves[flip]
        for g, (first, count) in enumerate(parts):
            piece = grp.at[pl.ds(first, count), side, piece_rows]
            if g == 0 and flip == 0:
                near = near_copies[part]

                @pl.when(half == 1)
                def _(piece=piece):
                    links.arrived(("grp", 0, part), piece, sibling)

                @pl.when(half == 0)
                def _():
                    near.wait()
            else:
                links.arrived(("grp", g, part), piece, sibling)
        dst = win.at[:, side, col, core, piece_rows]
        for by in others:
            src = grp.at[pl.ds(2 * col_up(by), slots), side, piece_rows]
            links.send(("win_x", by, part), src, dst, me_col[by])
        made = local(grp.at[pl.ds(2 * col, slots), side, piece_rows], dst)
        made.start()
        win_copies.append(made)
        if part == 3:
            src = grp.at[pl.ds(2 * col + 1 - core, nq)]
            links.send(("win_s", 0), src, win.at[pl.ds(1 - core, nq), :, col, core], sibling)

    def mirror():
        own_copy.wait()
        links.arrived(("own_s", 0), own.at[:, half, col, 1 - core], sibling)
        links.arrived(("own_sy", 0), own.at[:, 1 - half, col, 1 - core], sibling)
        for by in others:
            src_col = col_down(by)
            links.arrived(("own_sx", by), own.at[:, half, src_col, 1 - core], sibling)
            if split:
                piece = own.at[a_part, 1 - half, src_col, 1 - core]
                links.arrived(("own_sa", by), piece, sibling)
            if split < nq:
                piece = own.at[b_part, 1 - half, src_col, 1 - core]
                links.arrived(("own_sb", by), piece, sibling)
        for q in range(nq):
            block_copies[q].wait()

            def mirrored(n, carry, q=q):
                product = lax.dot_general(
                    blocks[q, :, tile_at(n)],
                    own[q].reshape(patches, width),
                    (((0,), (0,)), ((), ())),
                    preferred_element_type=F32,
                )
                mr[q, n] = product.reshape(
                    per_tile, 2, slice_rows, width
                )
                return carry

            lax.fori_loop(0, tiles, mirrored, 0, unroll=True)
            links.send(("ms", q), mr.at[q, :, :, 1 - core], ms.at[q], sibling)

    def unite():
        for i in range(slots):
            if i < nq:
                links.arrived(("ms", i), ms.at[i], sibling)
            if i == 0:

                @pl.when(core == 0)
                def _():
                    un[0] = mr[0, :, :, 0]

                @pl.when(core == 1)
                def _():
                    un[0] = ms[0]
            elif i == nq:

                @pl.when(core == 0)
                def _():
                    un[nq] = ms[nq - 1]

                @pl.when(core == 1)
                def _():
                    un[nq] = mr[nq - 1, :, :, 1]
            else:
                un[i] = mr[i - core, :, :, core] + ms[i - 1 + core]

    def sums_send(part):
        flip, piece_rows = sum_parts[part]
        side = halves[flip]
        for by in others:
            src = un.at[:, side, col_up(by), piece_rows]
            links.send(("mx", by, part), src, mx.at[by - 1, :, side, piece_rows], me_col[by])

    def opposite_pass():
        for side in range(2):
            piece = rf.at[:, side, core]
            links.arrived(("rf", 0), piece, sibling, side)
            links.send(("rf_s", 0), piece, piece, sibling, side)

    def window_pass():
        for by in others:
            src_col = col_down(by)
            for part, (flip, piece_rows) in enumerate(reach_parts):
                piece = win.at[:, halves[flip], src_col, core, piece_rows]
                links.arrived(("win_x", by, part), piece, sibling)
            piece = win.at[pl.ds(1 - core, nq), :, src_col, core]
            links.send(("win_s", by), piece, piece, sibling)

    def forward(q):
        if q == 0:
            for made in win_copies:
                made.wait()
            for by in range(columns):
                piece = win.at[pl.ds(core, nq), :, col_down(by), 1 - core]
                links.arrived(("win_s", by), piece, sibling)

        def forwarded(n, carry):
            product = jnp.dot(
                blocks[q, tile_at(n), :],
                win[core + q].reshape(patches, width),
                preferred_element_type=F32,
            )
            fw[q, n] = product.reshape(per_tile, 2, slice_rows, width)
            return carry

        lax.fori_loop(0, tiles, forwarded, 0, unroll=True)
        links.send(("fs", q), fw.at[q, :, :, 1 - core], fs.at[q], sibling)

    def forward_unite(q):
        links.arrived(("fs", q), fs.at[q], sibling)
        fw[q, :, :, core] = fw[q, :, :, core] + fs[q]

        @pl.when((half == 0) & (2 * col <= q))
        def _():
            fw[q, :, :, core] = fw[q, :, :, core] + un[q - 2 * col]

        if q not in XFIRST:
            links.send(("fy", q), fw.at[q, 1 - half, :, core], fy.at[q], partner)

    def opposite(q):
        if q == 0:
            for side in range(2):
                far_copies[side].wait()
                links.arrived(("rf_s", 0), rf.at[:, side, 1 - core], sibling, side)
                for by in others:
                    links.arrived(("far", by, side), fbuf.at[side, :, col_down(by)], sibling)
        depth = 2 * slice_rows
        product = sum(
            jnp.dot(
                fbuf[side, q].reshape(columns * slice_rows, depth),
                rf[q, side].reshape(depth, width),
                preferred_element_type=F32,
            )
            for side in range(2)
        )
        fw[q, half, :, core] = fw[q, half, :, core] + product.reshape(columns, slice_rows, width)
        if q in XFIRST:
            for by in others:
                links.send(("fx", by, q), fw.at[q, :, col_up(by), core], fx.at[by - 1, q], me_col[by])

    def forward_pass(q):
        if q in XFIRST:
            total = fw[q, :, col, core]
            for by in others:
                links.arrived(("fx", by, q), fx.at[by - 1, q], sibling)
                total = total + fx[by - 1, q]
            fw[q, :, col, core] = total
            links.send(("fy", q), fw.at[q, 1 - half, col, core], fy.at[q, 0], partner)
        else:
            links.arrived(("fy", q), fy.at[q], partner)
            fw[q, half, :, core] = fw[q, half, :, core] + fy[q]
            for by in others:
                links.send(
                    ("fx", by, q),
                    fw.at[q, half, col_up(by), core],
                    fx.at[by - 1, q, half],
                    me_col[by],
                )

    def forward_end(q):
        if q in XFIRST:
            links.arrived(("fy", q), fy.at[q, 0], partner)
            out[q] = fw[q, half, col, core] + fy[q, 0]
        else:
            total = fw[q, half, col, core]
            for by in others:
                links.arrived(("fx", by, q), fx.at[by - 1, q, half], sibling)
                total = total + fx[by - 1, q, half]
            out[q] = total

    def sums_pass(part):
        flip, piece_rows = sum_parts[part]
        side = halves[flip]
        hz_own[:, side, piece_rows] = jnp.zeros((groups, part_rows, width), F32)
        hz_own[pl.ds(2 * col, slots), side, piece_rows] = un[:, side, col, piece_rows]
        for by in others:
            links.arrived(("mx", by, part), mx.at[by - 1, :, side, piece_rows], sibling)
            reach = pl.ds(2 * col_down(by), slots)
            hz_own[reach, side, piece_rows] = (
                hz_own[reach, side, piece_rows] + mx[by - 1, :, side, piece_rows]
            )
        for g, (first, count) in enumerate(parts):
            src = hz_own.at[pl.ds(first, count), side, piece_rows]
            dst = hz.at[half, pl.ds(first, count), piece_rows]
            target = at(row_up(start_of(half) + g), side, col, core)
            remote = links.copy(("hz", g, part), src, dst, target)
            if g == 0:
                conditional.append(remote)

                @pl.when(half == 1)
                def _(remote=remote):
                    remote.start()
            else:
                remote.start()

    scope = locals()
    for step in ORDER:
        name, *args = step.split()
        scope[name](*map(int, args))

    for made in small_copies:
        made.wait()
    kinds, bands = tab.shape
    reflect_of = jnp.concatenate([tab[...]] * (width // bands), axis=1)
    across = lax.broadcasted_iota(jnp.int32, (slice_rows, slice_rows), 1)
    down = lax.broadcasted_iota(jnp.int32, (slice_rows, slice_rows), 0)

    def upright(values):
        spread = jnp.broadcast_to(values, (slice_rows, slice_rows))
        return jnp.sum(jnp.where(across == down, spread, 0), axis=1, keepdims=True)

    for q in range(nq):
        kind = upright(mat[pl.ds(q, 1), :])
        reflect = jnp.zeros((slice_rows, width), F32)
        for m in range(kinds):
            reflect = jnp.where(kind == m, reflect_of[m : m + 1, :], reflect)
        refl[q] = reflect

    def sends_end(some):
        for made in some:
            if any(made is other for other in conditional):

                @pl.when(half == 1)
                def _(made=made):
                    made.wait_send()
            else:
                made.wait_send()

    late = len(others) + len(parts)
    sends_end(links.sent[:-late])
    for q in range(nq):
        forward_end(q)
    for part, (flip, piece_rows) in enumerate(sum_parts):
        for g, (first, count) in enumerate(parts):
            piece = hz.at[halves[flip], pl.ds(first, count), piece_rows]
            if g == 0:

                @pl.when(halves[flip] == 1)
                def _(piece=piece, part=part):
                    links.arrived(("hz", 0, part), piece, sibling)
            else:
                links.arrived(("hz", g, part), piece, sibling)
    result_copies = []
    for q in range(nq):
        total = out[q]
        for half_from in range(2):
            for u in range(q + (0 if half_from else nq), groups, nq):
                total = total + hz[half_from, u]
        irradiation = total / upright(area[pl.ds(q, 1), :])
        out[q] = emi_v[q].astype(F32) + refl[q] * irradiation
        made = local(out.at[q], result.at[q])
        made.start()
        result_copies.append(made)
    sends_end(links.sent[-late:])
    for made in result_copies:
        made.wait()


def on_device(rows, columns, radiosity, emission, areas, patch_material, reflect_table, pair_blocks, far_blocks):
    nq, slice_rows, width = radiosity.shape
    patches = pair_blocks.shape[2]
    slots = nq + 1
    groups = 2 * columns + nq - 1
    bf16 = jnp.bfloat16
    scratch = [
        pltpu.VMEM((nq, patches, patches), bf16),
        pltpu.VMEM((nq, 2, columns, 2, slice_rows, width), bf16),
        pltpu.VMEM((slots, 2, columns, 2, slice_rows, width), bf16),
        pltpu.VMEM((groups, 2, slice_rows, width), bf16),
        pltpu.VMEM((2, nq, columns, slice_rows, 2 * slice_rows), bf16),
        pltpu.VMEM((nq, 2, 2, slice_rows, width), bf16),
        pltpu.VMEM((nq, 2, columns, 2, slice_rows, width), F32),
        pltpu.VMEM((nq, 2, columns, slice_rows, width), F32),
        pltpu.VMEM((nq, columns, slice_rows, width), F32),
        pltpu.VMEM((columns - 1, nq, 2, slice_rows, width), F32),
        pltpu.VMEM((nq, 2, columns, 2, slice_rows, width), F32),
        pltpu.VMEM((nq, 2, columns, slice_rows, width), F32),
        pltpu.VMEM((slots, 2, columns, slice_rows, width), F32),
        pltpu.VMEM((columns - 1, slots, 2, slice_rows, width), F32),
        pltpu.VMEM((groups, 2, slice_rows, width), F32),
        pltpu.VMEM((2, groups, slice_rows, width), F32),
        pltpu.VMEM((nq, slice_rows, width), bf16),
        pltpu.VMEM((nq, slice_rows, width), F32),
        pltpu.VMEM(areas.shape, F32),
        pltpu.VMEM(patch_material.shape, jnp.int32),
        pltpu.VMEM(reflect_table.shape, F32),
        pltpu.VMEM((nq, slice_rows, width), F32),
        pltpu.SemaphoreType.DMA((160,)),
        pltpu.SemaphoreType.DMA((160,)),
        pltpu.SemaphoreType.DMA((24,)),
    ]
    any_space = pl.BlockSpec(memory_space=pl.ANY)
    flops = 4 * nq * patches * patches * width
    return pl.pallas_call(
        functools.partial(kernel, rows, columns),
        out_shape=jax.ShapeDtypeStruct((nq, slice_rows, width), F32),
        in_specs=[any_space] * 7,
        out_specs=any_space,
        scratch_shapes=scratch,
        compiler_params=pltpu.CompilerParams(
            collective_id=0, has_side_effects=True, vmem_limit_bytes=58 * 2**20
        ),
        cost_estimate=pl.CostEstimate(
            flops=flops, bytes_accessed=2 * nq * patches * patches, transcendentals=0
        ),
    )(radiosity, emission, areas, patch_material, reflect_table, pair_blocks, far_blocks)


def solution(mesh):
    rows, stops = mesh.shape["row"], mesh.shape["stop"]
    return jax.shard_map(
        functools.partial(on_device, rows, stops // 4),
        mesh=mesh,
        in_specs=(
            P("row", "stop", None),
            P("row", "stop", None),
            P("row", "stop"),
            P("row", "stop"),
            P(),
            P("row", "stop", None, None),
            P("row", "stop", None),
        ),
        out_specs=P("row", "stop", None),
        check_vma=False,
    )
```

```python
import functools

import jax
import jax.numpy as jnp
from jax import lax
from jax.experimental import pallas as pl
from jax.experimental.pallas import tpu as pltpu
from jax.sharding import PartitionSpec as P

MESH = pl.DeviceIdType.MESH
F32 = jnp.float32


SPLIT = 0
XFIRST = ()
ORDER = (
    "own_send",
    "reach_send 0",
    "reach_send 1",
    "reach_send 2",
    "reach_send 3",
    "own_pass_y",
    "own_pass_x",
    "reach_pass 0",
    "reach_pass 1",
    "own_end",
    "reach_pass 2",
    "mirror",
    "reach_pass 3",
    "opposite_send",
    "unite",
    "opposite_pass",
    "window_pass",
    "sums_send 0",
    "sums_send 1",
    "far_send",
    "sums_send 2",
    "forward 0",
    "forward 1",
    "forward_unite 0",
    "forward 2",
    "forward_unite 1",
    "forward 3",
    "forward_unite 2",
    "forward_unite 3",
    "sums_pass 0",
    "sums_send 3",
    "opposite 0",
    "opposite 1",
    "opposite 2",
    "opposite 3",
    "forward_pass 0",
    "sums_pass 1",
    "forward_pass 1",
    "sums_pass 2",
    "forward_pass 2",
    "sums_pass 3",
    "forward_pass 3",
)


class Links:
    def __init__(self, send_sem, recv_sem):
        self.send_sem, self.recv_sem = send_sem, recv_sem
        self.names, self.recv_count, self.sent = {}, 0, []

    def name(self, key, count=1):
        self.names[key] = self.recv_count
        self.recv_count += count

    def copy(self, key, src, dst, target, extra=0):
        made = pltpu.make_async_remote_copy(
            src_ref=src,
            dst_ref=dst,
            send_sem=self.send_sem.at[len(self.sent)],
            recv_sem=self.recv_sem.at[self.names[key] + extra],
            device_id=target,
            device_id_type=MESH,
        )
        self.sent.append(made)
        return made

    def send(self, key, src, dst, target, extra=0):
        self.copy(key, src, dst, target, extra).start()

    def arrived(self, key, dst, target, extra=0):
        pltpu.make_async_remote_copy(
            src_ref=dst,
            dst_ref=dst,
            send_sem=self.send_sem.at[0],
            recv_sem=self.recv_sem.at[self.names[key] + extra],
            device_id=target,
            device_id_type=MESH,
        ).wait_recv()


def kernel(
    rows, columns,
    rad, emi, area_in, mat_in, tab_in, pair, far, result,
    blocks, own, win, grp, fbuf, rf, fw, fs, fy, fx, mr, ms, un, mx, hz_own, hz, emi_v, refl,
    area, mat, tab, out,
    send_sem, recv_sem, local_sem,
):
    nq, slice_rows, width = rad.shape
    patches = pair.shape[2]
    half_patches = patches // 2
    slots = nq + 1
    groups = 2 * columns + nq - 1
    parts = [(g * nq, min(nq, groups - g * nq)) for g in range(-(-groups // nq))]
    row, stop = lax.axis_index("row"), lax.axis_index("stop")
    half, col, core = stop // (2 * columns), (stop // 2) % columns, stop % 2
    others = range(1, columns)

    def at(row_by, half_to, col_to, core_to):
        return (row_by, half_to * (2 * columns) + col_to * 2 + core_to)

    def row_up(by):
        return lax.rem(row + by, rows)

    def row_down(by):
        return lax.rem(row + rows - by, rows)

    def col_up(by):
        return lax.rem(col + by, columns)

    def col_down(by):
        return lax.rem(col + columns - by, columns)

    sibling = at(row, half, col, 1 - core)
    partner = at(row, 1 - half, col, core)
    me_col = {by: at(row, half, col_up(by), core) for by in others}
    starts = (0, 2 * columns // nq)
    halves = (half, 1 - half)

    def start_of(which):
        return jnp.where(which == 0, starts[0], starts[1])

    split = SPLIT
    links = Links(send_sem, recv_sem)
    for by in others:
        for key in ("own_x", "own_sx", "own_ya", "own_xb", "own_sa", "own_sb"):
            links.name((key, by))
        for side in range(2):
            links.name(("far", by, side))
        for part in range(4):
            links.name(("mx", by, part))
            links.name(("win_x", by, part))
        for q in range(nq):
            links.name(("fx", by, q))
    for by in range(columns):
        links.name(("win_s", by))
    for key in ("own_s", "own_y", "own_sy"):
        links.name((key, 0))
    for key in ("rf", "rf_s"):
        links.name((key, 0), 2)
    for g in range(len(parts)):
        for part in range(4):
            links.name(("hz", g, part))
            links.name(("grp", g, part))
    for q in range(nq):
        for key in ("ms", "fs", "fy"):
            links.name((key, q))

    local_count = [0]

    def local(src, dst):
        made = pltpu.make_async_copy(src, dst, local_sem.at[local_count[0]])
        local_count[0] += 1
        return made

    def far_columns(side, column):
        first = side * half_patches + column * (2 * slice_rows)
        return pl.ds(pl.multiple_of(first, 2 * slice_rows), 2 * slice_rows)

    def offsets(mine, theirs):
        reach = {starts[mine] + g for g in range(len(parts))}
        back = {-(starts[theirs] + g) for g in range(len(parts))}
        both = {by % rows for by in reach | back | {rows // 2}}
        return sorted(both - {0} if mine == theirs else both)

    barrier = pltpu.get_barrier_semaphore()
    peers = []
    for a, b in zip(offsets(0, 1), offsets(1, 0), strict=True):
        peers.append(at(row_up(jnp.where(half == 0, a, b)), 1 - half, col, core))
    for a, b in zip(offsets(0, 0), offsets(1, 1), strict=True):
        peers.append(at(row_up(jnp.where(half == 0, a, b)), half, col, core))
    peers += [me_col[by] for by in others] + [sibling]
    for peer in peers:
        pl.semaphore_signal(barrier, inc=1, device_id=peer, device_id_type=MESH)

    own_copy = local(rad, own.at[:, half, col, core])
    own_copy.start()
    block_copies = []
    for q in range(nq):
        made = local(pair.at[q, 0], blocks.at[q])
        made.start()
        block_copies.append(made)
    far_copies = []
    for side in range(2):
        made = local(far.at[:, :, far_columns(side, col)], fbuf.at[side, :, col])
        made.start()
        far_copies.append(made)
    small_copies = []
    for src, dst in ((emi, emi_v), (area_in, area), (mat_in, mat), (tab_in, tab)):
        made = local(src, dst)
        made.start()
        small_copies.append(made)
    pl.semaphore_wait(barrier, len(peers))

    mine = own.at[:, half, col, core]
    win_copies, near_copies, conditional = [], [], []
    a_part, b_part = pl.ds(0, split), pl.ds(split, nq - split)
    per_tile = columns
    tile = per_tile * 2 * slice_rows
    tiles = patches // tile
    part_rows = slice_rows // 2
    row_parts = [pl.ds(n * part_rows, part_rows) for n in range(2)]
    sum_parts = [(flip, piece_rows) for flip in (1, 0) for piece_rows in row_parts]
    reach_parts = [(flip, piece_rows) for flip in (0, 1) for piece_rows in row_parts]

    def tile_at(n):
        return pl.ds(pl.multiple_of(n * tile, tile), tile)

    def own_send():
        links.send(("own_y", 0), rad, mine, partner)
        for by in others:
            links.send(("own_x", by), rad, mine, me_col[by])
        links.send(("own_s", 0), rad, mine, sibling)

    def reach_send(part):
        flip, piece_rows = reach_parts[part]
        for g, (first, count) in enumerate(parts):
            src = rad.at[pl.ds(0, count), piece_rows]
            dst = grp.at[pl.ds(first, count), half, piece_rows]
            source_row = row_down(start_of(halves[flip]) + g)
            target = at(source_row, halves[flip], col, core)
            remote = links.copy(("grp", g, part), src, dst, target)
            if g == 0 and flip == 0:
                near = local(src, dst)
                conditional.append(remote)
                near_copies.append(near)

                @pl.when(half == 1)
                def _(remote=remote):
                    remote.start()

                @pl.when(half == 0)
                def _(near=near):
                    near.start()
            else:
                remote.start()

    def opposite_send():
        for flip in range(2):
            target = at(row_down(rows // 2), halves[flip], col, core)
            links.send(("rf", 0), rad, rf.at[:, half, core], target, half)

    def far_send():
        for by in others:
            for side in range(2):
                src = far.at[:, :, far_columns(side, col_up(by))]
                links.send(("far", by, side), src, fbuf.at[side, :, col], me_col[by])

    def own_pass_y():
        piece = own.at[:, 1 - half, col, core]
        links.arrived(("own_y", 0), piece, partner)
        if split < nq:
            piece_b = own.at[b_part, 1 - half, col, core]
            for by in others:
                links.send(("own_xb", by), piece_b, piece_b, me_col[by])
        links.send(("own_sy", 0), piece, piece, sibling)

    def own_pass_x():
        for by in others:
            piece = own.at[:, half, col_down(by), core]
            links.arrived(("own_x", by), piece, me_col[by])
            if split:
                piece_a = own.at[a_part, half, col_down(by), core]
                links.send(("own_ya", by), piece_a, piece_a, partner)
            links.send(("own_sx", by), piece, piece, sibling)

    def own_end():
        for by in others:
            if split < nq:
                piece = own.at[b_part, 1 - half, col_down(by), core]
                links.arrived(("own_xb", by), piece, me_col[by])
                links.send(("own_sb", by), piece, piece, sibling)
            if split:
                piece = own.at[a_part, 1 - half, col_down(by), core]
                links.arrived(("own_ya", by), piece, partner)
                links.send(("own_sa", by), piece, piece, sibling)

    def reach_pass(part):
        flip, piece_rows = reach_parts[part]
        side = halves[flip]
        for g, (first, count) in enumerate(parts):
            piece = grp.at[pl.ds(first, count), side, piece_rows]
            if g == 0 and flip == 0:
                near = near_copies[part]

                @pl.when(half == 1)
                def _(piece=piece):
                    links.arrived(("grp", 0, part), piece, sibling)

                @pl.when(half == 0)
                def _():
                    near.wait()
            else:
                links.arrived(("grp", g, part), piece, sibling)
        dst = win.at[:, side, col, core, piece_rows]
        for by in others:
            src = grp.at[pl.ds(2 * col_up(by), slots), side, piece_rows]
            links.send(("win_x", by, part), src, dst, me_col[by])
        made = local(grp.at[pl.ds(2 * col, slots), side, piece_rows], dst)
        made.start()
        win_copies.append(made)
        if part == 3:
            src = grp.at[pl.ds(2 * col + 1 - core, nq)]
            links.send(("win_s", 0), src, win.at[pl.ds(1 - core, nq), :, col, core], sibling)

    def mirror():
        own_copy.wait()
        links.arrived(("own_s", 0), own.at[:, half, col, 1 - core], sibling)
        links.arrived(("own_sy", 0), own.at[:, 1 - half, col, 1 - core], sibling)
        for by in others:
            src_col = col_down(by)
            links.arrived(("own_sx", by), own.at[:, half, src_col, 1 - core], sibling)
            if split:
                piece = own.at[a_part, 1 - half, src_col, 1 - core]
                links.arrived(("own_sa", by), piece, sibling)
            if split < nq:
                piece = own.at[b_part, 1 - half, src_col, 1 - core]
                links.arrived(("own_sb", by), piece, sibling)
        for q in range(nq):
            block_copies[q].wait()

            def mirrored(n, carry, q=q):
                product = lax.dot_general(
                    blocks[q, :, tile_at(n)],
                    own[q].reshape(patches, width),
                    (((0,), (0,)), ((), ())),
                    preferred_element_type=F32,
                )
                mr[q, n] = product.reshape(
                    per_tile, 2, slice_rows, width
                )
                return carry

            lax.fori_loop(0, tiles, mirrored, 0, unroll=True)
            links.send(("ms", q), mr.at[q, :, :, 1 - core], ms.at[q], sibling)

    def unite():
        for i in range(slots):
            if i < nq:
                links.arrived(("ms", i), ms.at[i], sibling)
            if i == 0:

                @pl.when(core == 0)
                def _():
                    un[0] = mr[0, :, :, 0]

                @pl.when(core == 1)
                def _():
                    un[0] = ms[0]
            elif i == nq:

                @pl.when(core == 0)
                def _():
                    un[nq] = ms[nq - 1]

                @pl.when(core == 1)
                def _():
                    un[nq] = mr[nq - 1, :, :, 1]
            else:
                un[i] = mr[i - core, :, :, core] + ms[i - 1 + core]

    def sums_send(part):
        flip, piece_rows = sum_parts[part]
        side = halves[flip]
        for by in others:
            src = un.at[:, side, col_up(by), piece_rows]
            links.send(("mx", by, part), src, mx.at[by - 1, :, side, piece_rows], me_col[by])

    def opposite_pass():
        for side in range(2):
            piece = rf.at[:, side, core]
            links.arrived(("rf", 0), piece, sibling, side)
            links.send(("rf_s", 0), piece, piece, sibling, side)

    def window_pass():
        for by in others:
            src_col = col_down(by)
            for part, (flip, piece_rows) in enumerate(reach_parts):
                piece = win.at[:, halves[flip], src_col, core, piece_rows]
                links.arrived(("win_x", by, part), piece, sibling)
            piece = win.at[pl.ds(1 - core, nq), :, src_col, core]
            links.send(("win_s", by), piece, piece, sibling)

    def forward(q):
        if q == 0:
            for made in win_copies:
                made.wait()
            for by in range(columns):
                piece = win.at[pl.ds(core, nq), :, col_down(by), 1 - core]
                links.arrived(("win_s", by), piece, sibling)

        def forwarded(n, carry):
            product = jnp.dot(
                blocks[q, tile_at(n), :],
                win[core + q].reshape(patches, width),
                preferred_element_type=F32,
            )
            fw[q, n] = product.reshape(per_tile, 2, slice_rows, width)
            return carry

        lax.fori_loop(0, tiles, forwarded, 0, unroll=True)
        links.send(("fs", q), fw.at[q, :, :, 1 - core], fs.at[q], sibling)

    def forward_unite(q):
        links.arrived(("fs", q), fs.at[q], sibling)
        fw[q, :, :, core] = fw[q, :, :, core] + fs[q]

        @pl.when((half == 0) & (2 * col <= q))
        def _():
            fw[q, :, :, core] = fw[q, :, :, core] + un[q - 2 * col]

        if q not in XFIRST:
            links.send(("fy", q), fw.at[q, 1 - half, :, core], fy.at[q], partner)

    def opposite(q):
        if q == 0:
            for side in range(2):
                far_copies[side].wait()
                links.arrived(("rf_s", 0), rf.at[:, side, 1 - core], sibling, side)
                for by in others:
                    links.arrived(("far", by, side), fbuf.at[side, :, col_down(by)], sibling)
        depth = 2 * slice_rows
        product = sum(
            jnp.dot(
                fbuf[side, q].reshape(columns * slice_rows, depth),
                rf[q, side].reshape(depth, width),
                preferred_element_type=F32,
            )
            for side in range(2)
        )
        fw[q, half, :, core] = fw[q, half, :, core] + product.reshape(columns, slice_rows, width)
        if q in XFIRST:
            for by in others:
                links.send(("fx", by, q), fw.at[q, :, col_up(by), core], fx.at[by - 1, q], me_col[by])

    def forward_pass(q):
        if q in XFIRST:
            total = fw[q, :, col, core]
            for by in others:
                links.arrived(("fx", by, q), fx.at[by - 1, q], sibling)
                total = total + fx[by - 1, q]
            fw[q, :, col, core] = total
            links.send(("fy", q), fw.at[q, 1 - half, col, core], fy.at[q, 0], partner)
        else:
            links.arrived(("fy", q), fy.at[q], partner)
            fw[q, half, :, core] = fw[q, half, :, core] + fy[q]
            for by in others:
                links.send(
                    ("fx", by, q),
                    fw.at[q, half, col_up(by), core],
                    fx.at[by - 1, q, half],
                    me_col[by],
                )

    def forward_end(q):
        if q in XFIRST:
            links.arrived(("fy", q), fy.at[q, 0], partner)
            out[q] = fw[q, half, col, core] + fy[q, 0]
        else:
            total = fw[q, half, col, core]
            for by in others:
                links.arrived(("fx", by, q), fx.at[by - 1, q, half], sibling)
                total = total + fx[by - 1, q, half]
            out[q] = total

    def sums_pass(part):
        flip, piece_rows = sum_parts[part]
        side = halves[flip]
        hz_own[:, side, piece_rows] = jnp.zeros((groups, part_rows, width), F32)
        hz_own[pl.ds(2 * col, slots), side, piece_rows] = un[:, side, col, piece_rows]
        for by in others:
            links.arrived(("mx", by, part), mx.at[by - 1, :, side, piece_rows], sibling)
            reach = pl.ds(2 * col_down(by), slots)
            hz_own[reach, side, piece_rows] = (
                hz_own[reach, side, piece_rows] + mx[by - 1, :, side, piece_rows]
            )
        for g, (first, count) in enumerate(parts):
            src = hz_own.at[pl.ds(first, count), side, piece_rows]
            dst = hz.at[half, pl.ds(first, count), piece_rows]
            target = at(row_up(start_of(half) + g), side, col, core)
            remote = links.copy(("hz", g, part), src, dst, target)
            if g == 0:
                conditional.append(remote)

                @pl.when(half == 1)
                def _(remote=remote):
                    remote.start()
            else:
                remote.start()

    scope = locals()
    for step in ORDER:
        name, *args = step.split()
        scope[name](*map(int, args))

    for made in small_copies:
        made.wait()
    kinds, bands = tab.shape
    reflect_of = jnp.concatenate([tab[...]] * (width // bands), axis=1)
    across = lax.broadcasted_iota(jnp.int32, (slice_rows, slice_rows), 1)
    down = lax.broadcasted_iota(jnp.int32, (slice_rows, slice_rows), 0)

    def upright(values):
        spread = jnp.broadcast_to(values, (slice_rows, slice_rows))
        return jnp.sum(jnp.where(across == down, spread, 0), axis=1, keepdims=True)

    for q in range(nq):
        kind = upright(mat[pl.ds(q, 1), :])
        reflect = jnp.zeros((slice_rows, width), F32)
        for m in range(kinds):
            reflect = jnp.where(kind == m, reflect_of[m : m + 1, :], reflect)
        refl[q] = reflect

    def sends_end(some):
        for made in some:
            if any(made is other for other in conditional):

                @pl.when(half == 1)
                def _(made=made):
                    made.wait_send()
            else:
                made.wait_send()

    late = len(others) + len(parts)
    sends_end(links.sent[:-late])
    for q in range(nq):
        forward_end(q)
    for part, (flip, piece_rows) in enumerate(sum_parts):
        for g, (first, count) in enumerate(parts):
            piece = hz.at[halves[flip], pl.ds(first, count), piece_rows]
            if g == 0:

                @pl.when(halves[flip] == 1)
                def _(piece=piece, part=part):
                    links.arrived(("hz", 0, part), piece, sibling)
            else:
                links.arrived(("hz", g, part), piece, sibling)
    result_copies = []
    for q in range(nq):
        total = out[q]
        for half_from in range(2):
            for u in range(q + (0 if half_from else nq), groups, nq):
                total = total + hz[half_from, u]
        irradiation = total / upright(area[pl.ds(q, 1), :])
        out[q] = emi_v[q].astype(F32) + refl[q] * irradiation
        made = local(out.at[q], result.at[q])
        made.start()
        result_copies.append(made)
    sends_end(links.sent[-late:])
    for made in result_copies:
        made.wait()


def on_device(rows, columns, radiosity, emission, areas, patch_material, reflect_table, pair_blocks, far_blocks):
    nq, slice_rows, width = radiosity.shape
    patches = pair_blocks.shape[2]
    slots = nq + 1
    groups = 2 * columns + nq - 1
    bf16 = jnp.bfloat16
    scratch = [
        pltpu.VMEM((nq, patches, patches), bf16),
        pltpu.VMEM((nq, 2, columns, 2, slice_rows, width), bf16),
        pltpu.VMEM((slots, 2, columns, 2, slice_rows, width), bf16),
        pltpu.VMEM((groups, 2, slice_rows, width), bf16),
        pltpu.VMEM((2, nq, columns, slice_rows, 2 * slice_rows), bf16),
        pltpu.VMEM((nq, 2, 2, slice_rows, width), bf16),
        pltpu.VMEM((nq, 2, columns, 2, slice_rows, width), F32),
        pltpu.VMEM((nq, 2, columns, slice_rows, width), F32),
        pltpu.VMEM((nq, columns, slice_rows, width), F32),
        pltpu.VMEM((columns - 1, nq, 2, slice_rows, width), F32),
        pltpu.VMEM((nq, 2, columns, 2, slice_rows, width), F32),
        pltpu.VMEM((nq, 2, columns, slice_rows, width), F32),
        pltpu.VMEM((slots, 2, columns, slice_rows, width), F32),
        pltpu.VMEM((columns - 1, slots, 2, slice_rows, width), F32),
        pltpu.VMEM((groups, 2, slice_rows, width), F32),
        pltpu.VMEM((2, groups, slice_rows, width), F32),
        pltpu.VMEM((nq, slice_rows, width), bf16),
        pltpu.VMEM((nq, slice_rows, width), F32),
        pltpu.VMEM(areas.shape, F32),
        pltpu.VMEM(patch_material.shape, jnp.int32),
        pltpu.VMEM(reflect_table.shape, F32),
        pltpu.VMEM((nq, slice_rows, width), F32),
        pltpu.SemaphoreType.DMA((160,)),
        pltpu.SemaphoreType.DMA((160,)),
        pltpu.SemaphoreType.DMA((24,)),
    ]
    any_space = pl.BlockSpec(memory_space=pl.ANY)
    flops = 4 * nq * patches * patches * width
    return pl.pallas_call(
        functools.partial(kernel, rows, columns),
        out_shape=jax.ShapeDtypeStruct((nq, slice_rows, width), F32),
        in_specs=[any_space] * 7,
        out_specs=any_space,
        scratch_shapes=scratch,
        compiler_params=pltpu.CompilerParams(
            collective_id=0, has_side_effects=True, vmem_limit_bytes=58 * 2**20
        ),
        cost_estimate=pl.CostEstimate(
            flops=flops, bytes_accessed=2 * nq * patches * patches, transcendentals=0
        ),
    )(radiosity, emission, areas, patch_material, reflect_table, pair_blocks, far_blocks)


def solution(mesh):
    rows, stops = mesh.shape["row"], mesh.shape["stop"]
    return jax.shard_map(
        functools.partial(on_device, rows, stops // 4),
        mesh=mesh,
        in_specs=(
            P("row", "stop", None),
            P("row", "stop", None),
            P("row", "stop"),
            P("row", "stop"),
            P(),
            P("row", "stop", None, None),
            P("row", "stop", None),
        ),
        out_specs=P("row", "stop", None),
        check_vma=False,
    )
```
